512 devices in a mesh: tok: 16 (over z), exp: 32 (over y, x, core).
Axes of the slice: x: 4, y: 4, z: 16, core: 2. Of those that a mesh axis runs over, the one named last changes fastest.
Arguments:
- tokens: bfloat16 [4096, 4096], P('exp', 'tok'), may hold values from -6 to 6
- picked_blocks: int32 [8, 8], replicated, may hold values from 0 to 31, as said below
- gate_scale: float32 [8, 1024], replicated, may hold values from 0.1 to 1
- w_gate: bfloat16 [32, 4096, 2048], P('exp', None, 'tok'), may hold values from -0.09375 to 0.09375
- w_up: bfloat16 [32, 4096, 2048], P('exp', None, 'tok'), may hold values from -0.09375 to 0.09375
- w_down: bfloat16 [32, 2048, 4096], P('exp', None, 'tok'), may hold values from -0.0625 to 0.0625
Outputs:
- combined: bfloat16 [4096, 4096], P('exp', 'tok')
The draws below stay inside these ranges and needn't reach their ends.
Inputs may be any that keep to these rules, and one draw needn't show every extreme that they name: `picked_blocks`: each row names 8 different blocks, and every block is named by exactly two experts.
All inputs are finite; a program needn't handle non-finite values.
Results may differ from the reference program's by a relative error of at most 0.0049.
Values may be sent and summed in bfloat16 or wider, within the bound.
No kernel may reach another device: no remote copies, remote signals or barrier semaphores. Data moves between devices by JAX's collectives and lax.ppermute only.
A program may use at most 64 MiB of HBM per device.

```python
import math
import jax
import jax.numpy as jnp
from jax import lax

D = 4096
H = 8192
BLOCK = 128
SPAN = 4
CAPB = 8
EXPERTS = 8
NBLK = 32
TOKENS = 4096


def draw_picked_blocks(key, part):
    key = jax.random.fold_in(key, 7)
    first_order = jax.random.permutation(jax.random.fold_in(key, 1), NBLK)
    second_order = jax.random.permutation(jax.random.fold_in(key, 2), NBLK)
    joined = jnp.concatenate([first_order, second_order])
    return joined.reshape(EXPERTS, CAPB).astype(jnp.int32)


def level_of(stream_key, dims, cuts, least, high):
    gain = 1.0
    for position, blocks in cuts:
        steps = jax.random.uniform(jax.random.fold_in(jax.random.fold_in(stream_key, 6), position), (blocks,), jnp.float32, least / len(cuts), high / len(cuts))
        gain = gain * jnp.repeat(jnp.exp(steps), dims[position] // blocks).reshape((-1,) + (1,) * (len(dims) - 1 - position))
    return gain


def scatter_about(stream_key, dims, scale, reach, shards=(), dtype=jnp.bfloat16):
    level = level_of(stream_key, dims, shards, -0.22, 0.18) if shards else 1.0
    entries = jax.random.normal(stream_key, dims, jnp.float32) * scale * level
    return jnp.minimum(jnp.maximum(entries, -reach), reach).astype(dtype)


def setup_inputs(seed: int = 0) -> dict:
    streams_of = jax.random.split(jax.random.key(seed), 7)
    tokens = scatter_about(streams_of[0], (TOKENS, D), 1.0, 6.0, ((0, 32), (1, 16)))
    picked_blocks = draw_picked_blocks(jax.random.fold_in(streams_of[6], 71), 0)
    gate_scale = jnp.clip(jnp.exp(jax.random.uniform(streams_of[2], (EXPERTS, CAPB * BLOCK), jnp.float32, math.log(0.1), math.log(1.0))), 0.1, 1.0)
    w_gate = scatter_about(streams_of[3], (EXPERTS * SPAN, D, H // SPAN), D ** -0.5, 0.09375, ((0, 32), (2, 16)))
    w_up = scatter_about(streams_of[4], (EXPERTS * SPAN, D, H // SPAN), D ** -0.5, 0.09375, ((0, 32), (2, 16)))
    w_down = scatter_about(streams_of[5], (EXPERTS * SPAN, H // SPAN, D), H ** -0.5, 0.0625, ((0, 32), (2, 16)))
    return {"tokens": tokens, "picked_blocks": picked_blocks, "gate_scale": gate_scale, "w_gate": w_gate, "w_up": w_up, "w_down": w_down}


def reference(tokens, picked_blocks, gate_scale, w_gate, w_up, w_down):
    width = tokens.shape[1]
    blocked = tokens.reshape(NBLK, BLOCK, width)
    span_units = w_gate.shape[2]

    def per_expert(expert_id, total):
        chosen = lax.dynamic_index_in_dim(picked_blocks, expert_id, 0, keepdims=False)
        row_block = blocked[chosen].reshape(CAPB * BLOCK, width)
        first = (expert_id * SPAN).astype(jnp.int32)
        gate_mat = jnp.transpose(lax.dynamic_slice_in_dim(w_gate, first, SPAN, 0), (1, 0, 2)).reshape(width, SPAN * span_units)
        up_mat = jnp.transpose(lax.dynamic_slice_in_dim(w_up, first, SPAN, 0), (1, 0, 2)).reshape(width, SPAN * span_units)
        down_mat = lax.dynamic_slice_in_dim(w_down, first, SPAN, 0).reshape(SPAN * span_units, width)
        gate_sum = jnp.dot(row_block, gate_mat, preferred_element_type=jnp.float32)
        up_sum = jnp.dot(row_block, up_mat, preferred_element_type=jnp.float32)
        hidden = (jax.nn.silu(gate_sum) * up_sum).astype(jnp.bfloat16)
        scale_row = lax.dynamic_index_in_dim(gate_scale, expert_id, 0, keepdims=False)
        output_rows = jnp.dot(hidden, down_mat, preferred_element_type=jnp.float32) * scale_row[:, None]
        return total.at[chosen].add(output_rows.reshape(CAPB, BLOCK, width))

    start_total = jnp.zeros((NBLK, BLOCK, width), jnp.float32)
    total = lax.fori_loop(0, EXPERTS, per_expert, start_total)
    return total.reshape(TOKENS, width).astype(jnp.bfloat16)
```

```python
import jax
import jax.numpy as jnp
from jax import lax
from jax.experimental import pallas as pl
from jax.experimental.pallas import tpu as pltpu
from jax.sharding import PartitionSpec as P

BLOCK = 128
SPAN = 4
ACROSS = 4
CHIPS = 16
DEPTH = 16
OWNERS = 32
SAME_CORE = [[2 * chip + core for chip in range(CHIPS)] for core in range(2)]


def swap_core(value):
    return lax.ppermute(value, "exp", [(p, p ^ 1) for p in range(OWNERS)])


def partner_along(z, turn):
    if (z + turn) % 2 == 0:
        return (z + 1) % DEPTH
    return (z - 1) % DEPTH


def swap_depth(value, step):
    pairs = []
    for z in range(DEPTH):
        for p in range(OWNERS):
            pairs.append((z * OWNERS + p, partner_along(z, (step + p) % 2) * OWNERS + p))
    return lax.ppermute(value, ("tok", "exp"), pairs)


def gather_depth(chunk, odd):
    other = swap_depth(chunk, 0)
    pair = jnp.stack([jnp.where(odd, other, chunk), jnp.where(odd, chunk, other)])
    items = [pair]
    for step in range(1, DEPTH // 2):
        items.append(swap_depth(items[-1], step))
    return items


def pair_order(z, core):
    turned = lax.rem(z - core + DEPTH, DEPTH)
    pair, odd = turned // 2, lax.rem(turned, 2)
    away = jnp.where(odd == 1, 1, -1)
    pairs = [pair]
    for step in range(1, DEPTH // 2):
        reach = (step + 1) // 2
        pairs.append(pair + (away * reach if step % 2 else -away * reach))
    chunks = [2 * p + half + core for p in pairs for half in range(2)]
    return odd == 1, jnp.stack([lax.rem(chunk + 2 * DEPTH, DEPTH) for chunk in chunks]).astype(jnp.int32)


def hidden_kernel(order, *refs):
    items, weights, out = refs[: DEPTH // 2], refs[DEPTH // 2 : -1], refs[-1]
    sets = len(weights) // 2
    units = weights[0].shape[1]
    features = items[0].shape[2]
    total = None
    for number in range(DEPTH):
        rows = pl.ds(pl.multiple_of(order[number] * features, features), features)
        right = jnp.concatenate([w[rows, :] for w in weights], axis=1)
        term = jnp.dot(items[number // 2][number % 2], right, preferred_element_type=jnp.float32)
        total = term if total is None else total + term
    gate, up = total[:, : sets * units], total[:, sets * units :]
    out[...] = (gate / (1.0 + jnp.exp(-gate)) * up).astype(out.dtype)


def hidden_of(order, items, gates, ups):
    rows = items[0].shape[1]
    sets, units = len(gates), gates[0].shape[1]
    whole = pl.BlockSpec(memory_space=pltpu.VMEM)
    return pl.pallas_call(
        hidden_kernel,
        out_shape=jax.ShapeDtypeStruct((rows, sets * units), jnp.bfloat16),
        in_specs=[pl.BlockSpec(memory_space=pltpu.SMEM)] + [whole] * (len(items) + 2 * sets),
        out_specs=whole,
        compiler_params=pltpu.CompilerParams(vmem_limit_bytes=32 << 20),
        cost_estimate=pl.CostEstimate(
            flops=2 * rows * gates[0].shape[0] * 2 * sets * units,
            bytes_accessed=2 * sets * gates[0].size * 2,
            transcendentals=rows * sets * units,
        ),
        name="hidden",
    )(order, *items, *gates, *ups)


def down_kernel(order, *refs):
    items, scale, weights, out = refs[: DEPTH // 2], refs[DEPTH // 2], refs[DEPTH // 2 + 1 : -1], refs[-1]
    sets = len(weights)
    units = items[0].shape[2] // sets
    total = None
    for number in range(DEPTH):
        rows = pl.ds(pl.multiple_of(order[number] * units, units), units)
        right = jnp.concatenate([w[rows, :] for w in weights], axis=0)
        term = jnp.dot(items[number // 2][number % 2], right, preferred_element_type=jnp.float32)
        total = term if total is None else total + term
    out[...] = (total * scale[...]).astype(out.dtype)


def down_of(order, items, scale, downs):
    rows = items[0].shape[1]
    features = downs[0].shape[1]
    whole = pl.BlockSpec(memory_space=pltpu.VMEM)
    return pl.pallas_call(
        down_kernel,
        out_shape=jax.ShapeDtypeStruct((rows, features), jnp.bfloat16),
        in_specs=[pl.BlockSpec(memory_space=pltpu.SMEM)] + [whole] * (len(items) + 1 + len(downs)),
        out_specs=whole,
        compiler_params=pltpu.CompilerParams(vmem_limit_bytes=32 << 20),
        cost_estimate=pl.CostEstimate(
            flops=2 * rows * features * sum(w.shape[0] for w in downs),
            bytes_accessed=2 * sum(w.size for w in downs),
            transcendentals=0,
        ),
        name="down",
    )(order, *items, scale, *downs)


def shards(tokens, picked_blocks, gate_scale, w_gate, w_up, w_down):
    position = lax.axis_index("exp")
    z = lax.axis_index("tok")
    core = lax.rem(position, 2)
    expert = position // SPAN
    features = tokens.shape[1]
    chosen = lax.dynamic_index_in_dim(picked_blocks, expert, 0, keepdims=False)
    half = chosen.shape[0] // 2

    gates = [w_gate[0], swap_core(w_gate[0])]
    ups = [w_up[0], swap_core(w_up[0])]
    downs = [w_down[0], swap_core(w_down[0])]

    spread = jnp.broadcast_to(tokens[None], (CHIPS,) + tokens.shape)
    held = lax.all_to_all(spread, "exp", 0, 0, axis_index_groups=SAME_CORE, tiled=True)
    mine = lax.dynamic_slice_in_dim(chosen, core * half, half)
    theirs = lax.dynamic_slice_in_dim(chosen, (1 - core) * half, half)
    lent = swap_core(held[theirs // 2])
    here = (lax.rem(mine, 2) == core)[:, None, None]
    selected = jnp.where(here, held[mine // 2], lent)

    odd, order = pair_order(z, core)
    scale = lax.dynamic_index_in_dim(gate_scale, expert, 0, keepdims=False).reshape(2, 2, -1, 1)
    scale = lax.dynamic_index_in_dim(scale, core, 0, keepdims=False)
    parts = []
    for part in range(2):
        rows = selected[part * half // 2 : (part + 1) * half // 2].reshape(-1, features)
        hidden = hidden_of(order, gather_depth(rows, odd), gates, ups)
        parts.append(down_of(order, gather_depth(hidden, odd), scale[part], downs))
    done = jnp.concatenate(parts).reshape(half, BLOCK, features)

    others = swap_core(done)
    all_done = jnp.concatenate([done, others])
    names = jnp.concatenate([mine, theirs])
    match = names[None, :] == (2 * jnp.arange(CHIPS, dtype=jnp.int32) + core)[:, None]
    outgoing = jnp.where(match.any(1)[:, None, None], all_done[jnp.argmax(match, 1)], 0)
    arrived = lax.all_to_all(outgoing, "exp", 0, 0, axis_index_groups=SAME_CORE, tiled=True)
    return jnp.sum(arrived, axis=0, dtype=jnp.float32).astype(jnp.bfloat16)


def solution(mesh):
    return jax.shard_map(
        shards,
        mesh=mesh,
        in_specs=(
            P("exp", "tok"),
            P(),
            P(),
            P("exp", None, "tok"),
            P("exp", None, "tok"),
            P("exp", None, "tok"),
        ),
        out_specs=P("exp", "tok"),
        check_vma=False,
    )
```

```python
import functools

import jax
import jax.numpy as jnp
from jax import lax
from jax.experimental import pallas as pl
from jax.experimental.pallas import tpu as pltpu
from jax.sharding import PartitionSpec as P

BLOCK = 128
SPAN = 4
CHIPS = 16
DEPTH = 16
OWNERS = 32
PARTS = 2
SAME_CORE = [[2 * chip + core for chip in range(CHIPS)] for core in range(2)]


def swap_core(value):
    return lax.ppermute(value, "exp", [(p, p ^ 1) for p in range(OWNERS)])


def partner_along(z, turn):
    if (z + turn) % 2 == 0:
        return (z + 1) % DEPTH
    return (z - 1) % DEPTH


def swap_depth(value, step):
    pairs = []
    for z in range(DEPTH):
        for p in range(OWNERS):
            pairs.append((z * OWNERS + p, partner_along(z, (step + p) % 2) * OWNERS + p))
    return lax.ppermute(value, ("tok", "exp"), pairs)


def pair_order(z, core):
    turned = lax.rem(z - core + DEPTH, DEPTH)
    pair, odd = turned // 2, lax.rem(turned, 2)
    away = jnp.where(odd == 1, 1, -1)
    pairs = [pair]
    for step in range(1, DEPTH // 2):
        reach = (step + 1) // 2
        pairs.append(pair + (away * reach if step % 2 else -away * reach))
    chunks = [
        jnp.stack([lax.rem(2 * p + half + core + 2 * DEPTH, DEPTH) for half in range(2)]).astype(jnp.int32)
        for p in pairs
    ]
    return odd == 1, chunks


def step_kernel(join, first, finish, weight_count, order, pair, *refs):
    weights, rest = refs[:weight_count], list(refs[weight_count:])
    begun = None if first else rest.pop(0)
    scale = rest.pop(0) if finish == "scale" else None
    out, held, arrived = rest
    taken = held.shape[2]
    copies = []
    for half in range(2):
        rows = pl.ds(pl.multiple_of(order[half] * taken, taken), taken)
        for number, weight in enumerate(weights):
            copy = pltpu.make_async_copy(weight.at[rows, :], held.at[half, number], arrived.at[half, number])
            copy.start()
            copies.append(copy)
    total = None if first else begun[...]
    for half in range(2):
        for copy in copies[half * weight_count : (half + 1) * weight_count]:
            copy.wait()
        right = jnp.concatenate([held[half, number] for number in range(weight_count)], axis=join)
        term = jnp.dot(pair[half], right, preferred_element_type=jnp.float32)
        total = term if total is None else total + term
    if finish == "silu":
        units = total.shape[1] // 2
        gate, up = total[:, :units], total[:, units:]
        total = gate / (1.0 + jnp.exp(-gate)) * up
    elif finish == "scale":
        total = total * scale[...]
    out[...] = total.astype(out.dtype)


def add_product(order, pair, weights, join, begun, finish="", scale=None):
    _, rows, depth = pair.shape
    count = len(weights)
    taken = depth if join == 1 else depth // count
    columns = weights[0].shape[1] * (count if join == 1 else 1)
    width = columns // 2 if finish == "silu" else columns
    extra = ([] if begun is None else [begun]) + ([] if scale is None else [scale])
    return pl.pallas_call(
        functools.partial(step_kernel, join, begun is None, finish, count),
        out_shape=jax.ShapeDtypeStruct((rows, width), jnp.bfloat16 if finish else jnp.float32),
        in_specs=[pl.BlockSpec(memory_space=pltpu.SMEM), pl.BlockSpec(memory_space=pltpu.VMEM)]
        + [pl.BlockSpec(memory_space=pltpu.HBM)] * count
        + [pl.BlockSpec(memory_space=pltpu.VMEM)] * len(extra),
        out_specs=pl.BlockSpec(memory_space=pltpu.VMEM),
        scratch_shapes=[
            pltpu.VMEM((2, count, taken, weights[0].shape[1]), jnp.bfloat16),
            pltpu.SemaphoreType.DMA((2, count)),
        ],
        compiler_params=pltpu.CompilerParams(vmem_limit_bytes=16 << 20),
        cost_estimate=pl.CostEstimate(
            flops=2 * 2 * rows * depth * columns,
            bytes_accessed=2 * 2 * (rows * depth + depth * columns) + 8 * rows * columns,
            transcendentals=0,
        ),
        name="add_product",
    )(order, pair, *[pltpu.with_memory_space_constraint(w, pltpu.HBM) for w in weights], *extra)


def gathered_product(chunk, odd, orders, weights, join, finish, scale=None):
    other = swap_depth(chunk, 0)
    pair = jnp.stack([jnp.where(odd, other, chunk), jnp.where(odd, chunk, other)])
    total = None
    for step, order in enumerate(orders):
        last = step + 1 == len(orders)
        following = None if last else swap_depth(pair, step + 1)
        total = add_product(order, pair, weights, join, total, finish if last else "", scale if last else None)
        if not last:
            following, total = lax.optimization_barrier((following, total))
        pair = following
    return total


def shards(tokens, picked_blocks, gate_scale, w_gate, w_up, w_down):
    position = lax.axis_index("exp")
    z = lax.axis_index("tok")
    core = lax.rem(position, 2)
    expert = position // SPAN
    features = tokens.shape[1]
    chosen = lax.dynamic_index_in_dim(picked_blocks, expert, 0, keepdims=False)
    half = chosen.shape[0] // 2
    part_rows = BLOCK // PARTS

    ins = [w_gate[0], swap_core(w_gate[0]), w_up[0], swap_core(w_up[0])]
    downs = [w_down[0], swap_core(w_down[0])]

    odd, orders = pair_order(z, core)
    mine = lax.dynamic_slice_in_dim(chosen, core * half, half)
    theirs = lax.dynamic_slice_in_dim(chosen, (1 - core) * half, half)
    here = (lax.rem(mine, 2) == core)[:, None, None]
    scale = lax.dynamic_index_in_dim(gate_scale, expert, 0, keepdims=False).reshape(2, half, PARTS, part_rows)
    scale = lax.dynamic_index_in_dim(scale, core, 0, keepdims=False)
    names = jnp.concatenate([mine, theirs])
    match = names[None, :] == (2 * jnp.arange(CHIPS, dtype=jnp.int32) + core)[:, None]
    wanted, source = match.any(1)[:, None, None], jnp.argmax(match, 1)

    results = []
    for part in range(PARTS):
        own = tokens[part * part_rows : (part + 1) * part_rows]
        spread = jnp.broadcast_to(own[None], (CHIPS,) + own.shape)
        held = lax.all_to_all(spread, "exp", 0, 0, axis_index_groups=SAME_CORE, tiled=True)
        lent = swap_core(held[theirs // 2])
        rows = jnp.where(here, held[mine // 2], lent).reshape(-1, features)
        rows, ins, downs = lax.optimization_barrier((rows, ins, downs))
        hidden = gathered_product(rows, odd, orders, ins, 1, "silu")
        done = gathered_product(hidden, odd, orders, downs, 0, "scale", scale[:, part].reshape(-1, 1))
        done = done.reshape(half, part_rows, features)
        all_done = jnp.concatenate([done, swap_core(done)])
        outgoing = jnp.where(wanted, all_done[source], 0)
        arrived = lax.all_to_all(outgoing, "exp", 0, 0, axis_index_groups=SAME_CORE, tiled=True)
        results.append(jnp.sum(arrived, axis=0, dtype=jnp.float32).astype(jnp.bfloat16))
    return jnp.concatenate(results)


def solution(mesh):
    return jax.shard_map(
        shards,
        mesh=mesh,
        in_specs=(
            P("exp", "tok"),
            P(),
            P(),
            P("exp", None, "tok"),
            P("exp", None, "tok"),
            P("exp", None, "tok"),
        ),
        out_specs=P("exp", "tok"),
        check_vma=False,
    )
```

```python
import jax
import jax.numpy as jnp
from jax import lax
from jax.experimental import pallas as pl
from jax.experimental.pallas import tpu as pltpu
from jax.sharding import PartitionSpec as P

BLOCK = 128
SPAN = 4
CHIPS = 16
DEPTH = 16
OWNERS = 32
SAME_CORE = [[2 * chip + core for chip in range(CHIPS)] for core in range(2)]
TURNS = (15, 4, 2, 1)
MASKS = [0]
for turn in TURNS:
    MASKS += [mask ^ turn for mask in MASKS]


def swap_core(value):
    return lax.ppermute(value, "exp", [(p, p ^ 1) for p in range(OWNERS)])


def swap_across(value):
    return lax.ppermute(value, "exp", [(p, p ^ 2) for p in range(OWNERS)])


def swap_tok(value, partner):
    pairs = [(z * OWNERS + p, partner(z, p % 2) * OWNERS + p) for z in range(DEPTH) for p in range(OWNERS)]
    return lax.ppermute(value, ("tok", "exp"), pairs)


def swap_near(value, step):
    def partner(z, core):
        return (z + 1) % DEPTH if (z + step + core) % 2 == 0 else (z - 1) % DEPTH

    return swap_tok(value, partner)


def swap_turn(value, turn):
    return swap_tok(value, lambda z, core: (((z + 4 * core) % DEPTH ^ turn) - 4 * core) % DEPTH)


def near_order(z, core):
    turned = lax.rem(z - core + DEPTH, DEPTH)
    pair, odd = turned // 2, lax.rem(turned, 2)
    away = jnp.where(odd == 1, 1, -1)
    pairs = [pair]
    for step in range(1, DEPTH // 2):
        reach = (step + 1) // 2
        pairs.append(pair + (away * reach if step % 2 else -away * reach))
    chunks = [2 * p + half + core for p in pairs for half in range(2)]
    return odd == 1, lax.rem(jnp.stack(chunks) + 2 * DEPTH, DEPTH).astype(jnp.int32)


def turn_order(z, core):
    place = lax.rem(z + 4 * core, DEPTH)
    places = jnp.bitwise_xor(place, jnp.array(MASKS, jnp.int32))
    return lax.rem(places - 4 * core + DEPTH, DEPTH).astype(jnp.int32)


def start_rows(order, weights, held, arrived):
    taken = held.shape[2]
    copies = []
    for number in range(DEPTH):
        rows = pl.ds(pl.multiple_of(order[number] * taken, taken), taken)
        for which, weight in enumerate(weights):
            copy = pltpu.make_async_copy(weight.at[rows, :], held.at[number, which], arrived.at[number, which])
            copy.start()
            copies.append(copy)
    return copies


def hidden_kernel(order, first_low, first_high, second_low, second_high, *refs):
    ins, (out, held, arrived) = refs[:-3], refs[-3:]
    count = 2 * len(ins)
    weights = [w.at[kind] for kind in range(2) for w in ins]
    copies = start_rows(order, weights, held, arrived)
    total = None
    for number in range(DEPTH):
        first, second = (first_low, second_low) if number < DEPTH // 2 else (first_high, second_high)
        place = number % (DEPTH // 2)
        left = jnp.concatenate([first[place], second[place]], axis=0)
        for copy in copies[number * count : (number + 1) * count]:
            copy.wait()
        right = jnp.concatenate([held[number, which] for which in range(count)], axis=1)
        term = jnp.dot(left, right, preferred_element_type=jnp.float32)
        total = term if total is None else total + term
    units = total.shape[1] // 2
    gate, up = total[:, :units], total[:, units:]
    out[...] = (gate / (1.0 + jnp.exp(-gate)) * up).astype(out.dtype)


def down_kernel(order, scale, *refs):
    items, downs, (out, held, arrived) = refs[:DEPTH], refs[DEPTH:-3], refs[-3:]
    count = len(downs)
    copies = start_rows(order, downs, held, arrived)
    total = None
    for number in range(DEPTH):
        pair, half = number // 2, number % 2
        left = jnp.concatenate([items[pair][half], items[DEPTH // 2 + pair][half]], axis=0)
        for copy in copies[number * count : (number + 1) * count]:
            copy.wait()
        right = jnp.concatenate([held[number, which] for which in range(count)], axis=0)
        term = jnp.dot(left, right, preferred_element_type=jnp.float32)
        total = term if total is None else total + term
    out[...] = (total * scale[...]).astype(out.dtype)


def kernel_call(kernel, name, order, inner, weights, rows, columns, width, taken, count, wide):
    in_vmem = pl.BlockSpec(memory_space=pltpu.VMEM)
    return pl.pallas_call(
        kernel,
        out_shape=jax.ShapeDtypeStruct((rows, width), jnp.bfloat16),
        in_specs=[pl.BlockSpec(memory_space=pltpu.SMEM)]
        + [in_vmem] * len(inner)
        + [pl.BlockSpec(memory_space=pltpu.HBM)] * len(weights),
        out_specs=in_vmem,
        scratch_shapes=[
            pltpu.VMEM((DEPTH, count, taken, wide), jnp.bfloat16),
            pltpu.SemaphoreType.DMA((DEPTH, count)),
        ],
        compiler_params=pltpu.CompilerParams(vmem_limit_bytes=24 << 20),
        cost_estimate=pl.CostEstimate(
            flops=2 * rows * DEPTH * taken * count * wide,
            bytes_accessed=2 * DEPTH * taken * count * wide,
            transcendentals=0,
        ),
        name=name,
    )(order, *inner, *[pltpu.with_memory_space_constraint(w, pltpu.HBM) for w in weights])


def gather_half(chunk):
    held = chunk[None]
    for turn in TURNS[:-1]:
        held = jnp.concatenate([held, swap_turn(held, turn)])
    return held


def gather_near(chunk, odd):
    other = swap_near(chunk, 0)
    items = [jnp.stack([jnp.where(odd, other, chunk), jnp.where(odd, chunk, other)])]
    for step in range(1, DEPTH // 2):
        items.append(swap_near(items[-1], step))
    return items


def shards(tokens, picked_blocks, gate_scale, w_gate, w_up, w_down):
    position = lax.axis_index("exp")
    z = lax.axis_index("tok")
    core = lax.rem(position, 2)
    share = lax.rem(position, SPAN)
    expert = position // SPAN
    features = tokens.shape[1]
    chosen = lax.dynamic_index_in_dim(picked_blocks, expert, 0, keepdims=False)
    blocks = chosen.shape[0] // SPAN
    rows = blocks * BLOCK
    mine = lax.dynamic_slice_in_dim(chosen, blocks * share, blocks)
    theirs = lax.dynamic_slice_in_dim(chosen, blocks * jnp.bitwise_xor(share, 1), blocks)
    here = (lax.rem(mine, 2) == core)[:, None, None]
    odd, near = near_order(z, core)
    turns = turn_order(z, core)
    scale = lax.dynamic_index_in_dim(gate_scale, expert, 0, keepdims=False).reshape(SPAN, rows, 1)
    scale = lax.dynamic_index_in_dim(scale, share, 0, keepdims=False)
    names = jnp.concatenate([mine, theirs])
    match = names[None, :] == (2 * jnp.arange(CHIPS, dtype=jnp.int32) + core)[:, None]
    wanted, source = match.any(1)[:, None, None], jnp.argmax(match, 1)

    in_own = jnp.stack([w_gate[0], w_up[0]])
    down_own = w_down[0]
    spread = jnp.broadcast_to(tokens[None], (CHIPS,) + tokens.shape)
    held = lax.all_to_all(spread, "exp", 0, 0, axis_index_groups=SAME_CORE, tiled=True)
    in_near, down_near = swap_core(in_own), swap_core(down_own)
    held, in_own, down_own = lax.optimization_barrier((held, in_own, down_own))
    lent = swap_core(held[theirs // 2])
    selected = jnp.where(here, held[mine // 2], lent)
    selected, in_near, down_near, near, turns, wanted, source, odd, scale = lax.optimization_barrier(
        (selected, in_near, down_near, near, turns, wanted, source, odd, scale)
    )

    in_far = swap_across(in_own)
    lows = [gather_half(selected[block]) for block in range(blocks)]
    parts = [(low, swap_turn(low, TURNS[-1])) for low in lows]
    in_far, down_own, _ = lax.optimization_barrier((in_far, down_own, lows))
    down_far = swap_across(down_own)
    ins = [in_own, in_near, in_far, swap_core(in_far)]
    units = w_gate.shape[2]
    hidden = kernel_call(
        hidden_kernel, "hidden", turns, [p for part in parts for p in part], ins,
        rows, 2 * SPAN * units, SPAN * units, features, 2 * SPAN, units,
    )

    items = [item for block in range(blocks) for item in gather_near(hidden[block * BLOCK : (block + 1) * BLOCK], odd)]
    downs = [down_own, down_near, down_far, swap_core(down_far)]
    done = kernel_call(
        down_kernel, "down", near, [scale] + items, downs,
        rows, features, features, units, SPAN, features,
    )
    done = done.reshape(blocks, BLOCK, features)

    all_done = jnp.concatenate([done, swap_core(done)])
    outgoing = jnp.where(wanted, all_done[source], 0)
    arrived = lax.all_to_all(outgoing, "exp", 0, 0, axis_index_groups=SAME_CORE, tiled=True)
    return jnp.sum(arrived, axis=0, dtype=jnp.float32).astype(jnp.bfloat16)


def solution(mesh):
    return jax.shard_map(
        shards,
        mesh=mesh,
        in_specs=(
            P("exp", "tok"),
            P(),
            P(),
            P("exp", None, "tok"),
            P("exp", None, "tok"),
            P("exp", None, "tok"),
        ),
        out_specs=P("exp", "tok"),
        check_vma=False,
    )
```

```python
import jax
import jax.numpy as jnp
from jax import lax
from jax.experimental import pallas as pl
from jax.experimental.pallas import tpu as pltpu
from jax.sharding import PartitionSpec as P

BLOCK = 128
SPAN = 4
CHIPS = 16
DEPTH = 16
OWNERS = 32
SAME_CORE = [[2 * chip + core for chip in range(CHIPS)] for core in range(2)]
PAIRS = DEPTH // 2


def swap_core(value):
    return lax.ppermute(value, "exp", [(p, p ^ 1) for p in range(OWNERS)])


def swap_pair(value):
    return lax.ppermute(value, "tok", [(z, z ^ 1) for z in range(DEPTH)])


def swap_ring(value, step):
    route = []
    for z in range(DEPTH):
        for p in range(OWNERS):
            place = z // 2
            other = place + 1 if (place + step + p) % 2 == 0 else place - 1
            route.append((z * OWNERS + p, (other % PAIRS * 2 + z % 2) * OWNERS + p))
    return lax.ppermute(value, ("tok", "exp"), route)


def ring_order(place, core):
    turned = lax.rem(place - core + PAIRS, PAIRS)
    couple, odd = turned // 2, lax.rem(turned, 2)
    away = jnp.where(odd == 1, 1, -1)
    couples = [couple]
    for step in range(1, PAIRS // 2):
        reach = (step + 1) // 2
        couples.append(couple + (away * reach if step % 2 else -away * reach))
    places = [2 * c + half + core for c in couples for half in range(2)]
    return odd == 1, lax.rem(jnp.stack(places) + 2 * PAIRS, PAIRS).astype(jnp.int32)


def start_rows(order, sources, held, arrived):
    taken = held.shape[2]
    copies = []
    for number in range(DEPTH):
        for which, (weight, base) in enumerate(sources):
            rows = pl.ds(pl.multiple_of(order[number] * taken + base, taken), taken)
            copy = pltpu.make_async_copy(weight.at[rows, :], held.at[number, which], arrived.at[number, which])
            copy.start()
            copies.append(copy)
    return copies


def hidden_kernel(order, *refs):
    items, weights, (first, second, held, arrived) = refs[:PAIRS], refs[PAIRS:-4], refs[-4:]
    count = 2 * len(weights)
    copies = start_rows(order, [(w.at[kind], 0) for kind in range(2) for w in weights], held, arrived)
    total = None
    for number in range(DEPTH):
        couple, place, half = number // 4, number // 2 % 2, number % 2
        left = jnp.concatenate([items[couple][place, half], items[PAIRS // 2 + couple][place, half]], axis=0)
        for copy in copies[number * count : (number + 1) * count]:
            copy.wait()
        right = jnp.concatenate([held[number, which] for which in range(count)], axis=1)
        term = jnp.dot(left, right, preferred_element_type=jnp.float32)
        total = term if total is None else total + term
    units = total.shape[1] // 2
    gate, up = total[:, :units], total[:, units:]
    hidden = (gate / (1.0 + jnp.exp(-gate)) * up).astype(first.dtype)
    rows = first.shape[0]
    first[...] = hidden[:rows]
    second[...] = hidden[rows:]


def down_kernel(order, scale, *refs):
    items, weights, (kept, given, held, arrived) = refs[:PAIRS], refs[PAIRS:-4], refs[-4:]
    count = 2 * len(weights)
    depth = weights[0].shape[1] // 2
    copies = start_rows(order, [(w.at[2], side * depth) for w in weights for side in range(2)], held, arrived)
    total = None
    for number in range(PAIRS):
        couple, place = number // 2, number % 2
        left = jnp.concatenate([items[couple][place], items[PAIRS // 2 + couple][place]], axis=0)
        for copy in copies[2 * number * count : 2 * (number + 1) * count]:
            copy.wait()
        right = jnp.concatenate(
            [
                jnp.concatenate([held[2 * number + half, 2 * core + which] for which in (0, 1, 4, 5)], axis=1)
                for half in range(2)
                for core in range(2)
            ],
            axis=0,
        )
        term = jnp.dot(left, right, preferred_element_type=jnp.float32)
        total = term if total is None else total + term
    total = (total * scale[...]).astype(kept.dtype)
    columns = kept.shape[1]
    kept[...] = total[:, :columns]
    given[...] = total[:, columns:]


def kernel_call(kernel, name, order, inner, weights, outs, flops, taken):
    count, wide = 2 * len(weights), weights[0].shape[2]
    in_vmem = pl.BlockSpec(memory_space=pltpu.VMEM)
    return pl.pallas_call(
        kernel,
        out_shape=[jax.ShapeDtypeStruct(shape, jnp.bfloat16) for shape in outs],
        in_specs=[pl.BlockSpec(memory_space=pltpu.SMEM)]
        + [in_vmem] * len(inner)
        + [pl.BlockSpec(memory_space=pltpu.HBM)] * len(weights),
        out_specs=[in_vmem] * len(outs),
        scratch_shapes=[
            pltpu.VMEM((DEPTH, count, taken, wide), jnp.bfloat16),
            pltpu.SemaphoreType.DMA((DEPTH, count)),
        ],
        compiler_params=pltpu.CompilerParams(vmem_limit_bytes=24 << 20),
        cost_estimate=pl.CostEstimate(
            flops=flops,
            bytes_accessed=2 * DEPTH * taken * count * wide,
            transcendentals=0,
        ),
        name=name,
    )(order, *inner, *[pltpu.with_memory_space_constraint(w, pltpu.HBM) for w in weights])


def gather_ring(chunk, odd):
    other = swap_ring(chunk, 0)
    items = [jnp.stack([jnp.where(odd, other, chunk), jnp.where(odd, chunk, other)])]
    for step in range(1, PAIRS // 2):
        items.append(swap_ring(items[-1], step))
    return items


def shards(tokens, picked_blocks, gate_scale, w_gate, w_up, w_down):
    position = lax.axis_index("exp")
    z = lax.axis_index("tok")
    core, odd = lax.rem(position, 2), lax.rem(z, 2)
    expert = position // SPAN
    features, units = tokens.shape[1], w_gate.shape[2]
    chosen = lax.dynamic_index_in_dim(picked_blocks, expert, 0, keepdims=False)
    half = chosen.shape[0] // 2
    blocks = half // 2
    rows = blocks * BLOCK
    mine = lax.dynamic_slice_in_dim(chosen, half * core, half)
    theirs = lax.dynamic_slice_in_dim(chosen, half * (1 - core), half)
    here = (lax.rem(mine, 2) == core)[:, None, None]
    second, places = ring_order(z // 2, core)
    order_in = jnp.stack([2 * places, 2 * places + 1], axis=1).reshape(-1)
    order_down = jnp.stack([2 * places + odd, 2 * places + 1 - odd], axis=1).reshape(-1)
    scale = lax.dynamic_index_in_dim(gate_scale, expert, 0, keepdims=False).reshape(2, 2, rows, 1)
    scale = lax.dynamic_index_in_dim(scale, core, 0, keepdims=False)
    scale = lax.dynamic_index_in_dim(scale, odd, 0, keepdims=False)
    names = jnp.concatenate([mine, theirs])
    match = names[None, :] == (2 * jnp.arange(CHIPS, dtype=jnp.int32) + core)[:, None]
    wanted, source = match.any(1)[:, None, None], jnp.argmax(match, 1)

    spread = jnp.broadcast_to(tokens[None], (CHIPS,) + tokens.shape)
    spread, w_gate, w_up, w_down = lax.optimization_barrier((spread, w_gate, w_up, w_down))
    held = lax.all_to_all(spread, "exp", 0, 0, axis_index_groups=SAME_CORE, tiled=True)
    down = jnp.concatenate([w_down[0][:, :units], w_down[0][:, units:]])
    own = jnp.stack([w_gate[0], w_up[0], down])
    far = swap_pair(own)
    near = swap_core(own)
    lent = swap_core(held[theirs // 2])
    selected = jnp.where(here, held[mine // 2], lent)
    selected, near, order_in, order_down, wanted, source, second, scale = lax.optimization_barrier(
        (selected, near, order_in, order_down, wanted, source, second, scale)
    )

    selected = selected.reshape(2, rows, features)
    kept = lax.dynamic_index_in_dim(selected, odd, 0, keepdims=False)
    given = swap_pair(lax.dynamic_index_in_dim(selected, 1 - odd, 0, keepdims=False))
    both = jnp.stack([jnp.where(odd == 1, given, kept), jnp.where(odd == 1, kept, given)])
    chains = [gather_ring(both[:, block * BLOCK : (block + 1) * BLOCK], second) for block in range(blocks)]
    far, _ = lax.optimization_barrier((far, [chain[2] for chain in chains]))
    weights = [own, near, far, swap_core(far)]
    flops = 2 * rows * DEPTH * features * 2 * SPAN * units
    parts = kernel_call(
        hidden_kernel, "hidden", order_in, [item for chain in chains for item in chain], weights,
        [(BLOCK, SPAN * units)] * blocks, flops, features,
    )
    chains = [gather_ring(part, second) for part in parts]
    kept, given = kernel_call(
        down_kernel, "down", order_down, [scale] + [item for chain in chains for item in chain], weights,
        [(rows, features)] * 2, flops // 2, units,
    )
    given = swap_pair(given)
    done = jnp.stack([jnp.where(odd == 1, given, kept), jnp.where(odd == 1, kept, given)])
    done = done.reshape(half, BLOCK, features)

    all_done = jnp.concatenate([done, swap_core(done)])
    outgoing = jnp.where(wanted, all_done[source], 0)
    arrived = lax.all_to_all(outgoing, "exp", 0, 0, axis_index_groups=SAME_CORE, tiled=True)
    return jnp.sum(arrived, axis=0, dtype=jnp.float32).astype(jnp.bfloat16)


def solution(mesh):
    return jax.shard_map(
        shards,
        mesh=mesh,
        in_specs=(
            P("exp", "tok"),
            P(),
            P(),
            P("exp", None, "tok"),
            P("exp", None, "tok"),
            P("exp", None, "tok"),
        ),
        out_specs=P("exp", "tok"),
        check_vma=False,
    )
```

```python
import jax
import jax.numpy as jnp
from jax import lax
from jax.experimental import pallas as pl
from jax.experimental.pallas import tpu as pltpu
from jax.sharding import PartitionSpec as P

BLOCK = 128
SPAN = 4
ACROSS = 4
CHIPS = 16
DEPTH = 16
OWNERS = 32
SAME_CORE = [[2 * chip + core for chip in range(CHIPS)] for core in range(2)]


def swap_core(value):
    return lax.ppermute(value, "exp", [(p, p ^ 1) for p in range(OWNERS)])


def partner_along(z, turn):
    if (z + turn) % 2 == 0:
        return (z + 1) % DEPTH
    return (z - 1) % DEPTH


def swap_depth(value, step):
    pairs = []
    for z in range(DEPTH):
        for p in range(OWNERS):
            pairs.append((z * OWNERS + p, partner_along(z, (step + p) % 2) * OWNERS + p))
    return lax.ppermute(value, ("tok", "exp"), pairs)


def gather_depth(chunk, odd):
    other = swap_depth(chunk, 0)
    pair = jnp.stack([jnp.where(odd, other, chunk), jnp.where(odd, chunk, other)])
    items = [pair]
    for step in range(1, DEPTH // 2):
        items.append(swap_depth(items[-1], step))
    return items


def pair_order(z, core):
    turned = lax.rem(z - core + DEPTH, DEPTH)
    pair, odd = turned // 2, lax.rem(turned, 2)
    away = jnp.where(odd == 1, 1, -1)
    pairs = [pair]
    for step in range(1, DEPTH // 2):
        reach = (step + 1) // 2
        pairs.append(pair + (away * reach if step % 2 else -away * reach))
    chunks = [2 * p + half + core for p in pairs for half in range(2)]
    return odd == 1, jnp.stack([lax.rem(chunk + 2 * DEPTH, DEPTH) for chunk in chunks]).astype(jnp.int32)


def hidden_kernel(order, *refs):
    items, weights, out = refs[: DEPTH // 2], refs[DEPTH // 2 : -1], refs[-1]
    sets = len(weights) // 2
    units = weights[0].shape[1]
    features = items[0].shape[2]
    total = None
    for number in range(DEPTH):
        rows = pl.ds(pl.multiple_of(order[number] * features, features), features)
        right = jnp.concatenate([w[rows, :] for w in weights], axis=1)
        term = jnp.dot(items[number // 2][number % 2], right, preferred_element_type=jnp.float32)
        total = term if total is None else total + term
    gate, up = total[:, : sets * units], total[:, sets * units :]
    out[...] = (gate / (1.0 + jnp.exp(-gate)) * up).astype(out.dtype)


def hidden_of(order, items, gates, ups):
    rows = items[0].shape[1]
    sets, units = len(gates), gates[0].shape[1]
    whole = pl.BlockSpec(memory_space=pltpu.VMEM)
    return pl.pallas_call(
        hidden_kernel,
        out_shape=jax.ShapeDtypeStruct((rows, sets * units), jnp.bfloat16),
        in_specs=[pl.BlockSpec(memory_space=pltpu.SMEM)] + [whole] * (len(items) + 2 * sets),
        out_specs=whole,
        compiler_params=pltpu.CompilerParams(vmem_limit_bytes=16 << 20),
        cost_estimate=pl.CostEstimate(
            flops=2 * rows * gates[0].shape[0] * 2 * sets * units,
            bytes_accessed=2 * sets * gates[0].size * 2,
            transcendentals=rows * sets * units,
        ),
        name="hidden",
    )(order, *items, *gates, *ups)


def down_kernel(order, *refs):
    items, scale, weights, out = refs[: DEPTH // 2], refs[DEPTH // 2], refs[DEPTH // 2 + 1 : -1], refs[-1]
    sets = len(weights)
    units = items[0].shape[2] // sets
    total = None
    for number in range(DEPTH):
        rows = pl.ds(pl.multiple_of(order[number] * units, units), units)
        right = jnp.concatenate([w[rows, :] for w in weights], axis=0)
        term = jnp.dot(items[number // 2][number % 2], right, preferred_element_type=jnp.float32)
        total = term if total is None else total + term
    out[...] = (total * scale[:, :1]).astype(out.dtype)


def down_of(order, items, scale, downs):
    rows = items[0].shape[1]
    features = downs[0].shape[1]
    whole = pl.BlockSpec(memory_space=pltpu.VMEM)
    return pl.pallas_call(
        down_kernel,
        out_shape=jax.ShapeDtypeStruct((rows, features), jnp.bfloat16),
        in_specs=[pl.BlockSpec(memory_space=pltpu.SMEM)] + [whole] * (len(items) + 1 + len(downs)),
        out_specs=whole,
        compiler_params=pltpu.CompilerParams(vmem_limit_bytes=16 << 20),
        cost_estimate=pl.CostEstimate(
            flops=2 * rows * features * sum(w.shape[0] for w in downs),
            bytes_accessed=2 * sum(w.size for w in downs),
            transcendentals=0,
        ),
        name="down",
    )(order, *items, scale, *downs)


def shards(tokens, picked_blocks, gate_scale, w_gate, w_up, w_down):
    position = lax.axis_index("exp")
    z = lax.axis_index("tok")
    core = lax.rem(position, 2)
    expert = position // SPAN
    features = tokens.shape[1]
    chosen = lax.dynamic_index_in_dim(picked_blocks, expert, 0, keepdims=False)
    half = chosen.shape[0] // 2

    gates = [w_gate[0], swap_core(w_gate[0])]
    ups = [w_up[0], swap_core(w_up[0])]
    downs = [w_down[0], swap_core(w_down[0])]

    spread = jnp.broadcast_to(tokens[None], (CHIPS,) + tokens.shape)
    held = lax.all_to_all(spread, "exp", 0, 0, axis_index_groups=SAME_CORE, tiled=True)
    mine = lax.dynamic_slice_in_dim(chosen, core * half, half)
    theirs = lax.dynamic_slice_in_dim(chosen, (1 - core) * half, half)
    lent = swap_core(held[theirs // 2])
    here = (lax.rem(mine, 2) == core)[:, None, None]
    selected = jnp.where(here, held[mine // 2], lent)

    odd, order = pair_order(z, core)
    scale = lax.dynamic_index_in_dim(gate_scale, expert, 0, keepdims=False).reshape(2, 2, -1, 1)
    scale = lax.dynamic_index_in_dim(scale, core, 0, keepdims=False)
    scales = [jnp.broadcast_to(scale[part], (scale.shape[1], 128)) for part in range(2)]
    names = jnp.concatenate([mine, theirs])
    match = names[None, :] == (2 * jnp.arange(CHIPS, dtype=jnp.int32) + core)[:, None]
    wanted, source = match.any(1)[:, None, None], jnp.argmax(match, 1)
    selected, gates, ups, downs, odd, order, scales, wanted, source = lax.optimization_barrier(
        (selected, gates, ups, downs, odd, order, scales, wanted, source)
    )
    parts = []
    for part in range(2):
        rows = selected[part * half // 2 : (part + 1) * half // 2].reshape(-1, features)
        hidden = hidden_of(order, gather_depth(rows, odd), gates, ups)
        parts.append(down_of(order, gather_depth(hidden, odd), scales[part], downs))
    done = jnp.concatenate(parts).reshape(half, BLOCK, features)

    others = swap_core(done)
    all_done = jnp.concatenate([done, others])
    outgoing = jnp.where(wanted, all_done[source], 0)
    arrived = lax.all_to_all(outgoing, "exp", 0, 0, axis_index_groups=SAME_CORE, tiled=True)
    return jnp.sum(arrived, axis=0, dtype=jnp.float32).astype(jnp.bfloat16)


def solution(mesh):
    return jax.shard_map(
        shards,
        mesh=mesh,
        in_specs=(
            P("exp", "tok"),
            P(),
            P(),
            P("exp", None, "tok"),
            P("exp", None, "tok"),
            P("exp", None, "tok"),
        ),
        out_specs=P("exp", "tok"),
        check_vma=False,
    )
```

```python
import jax
import jax.numpy as jnp
from jax import lax
from jax.experimental import pallas as pl
from jax.experimental.pallas import tpu as pltpu
from jax.sharding import PartitionSpec as P

BLOCK = 128
SPAN = 4
CHIPS = 16
DEPTH = 16
OWNERS = 32
BLOCKS = 2
RELAY = 6
SAME_CORE = [[2 * chip + core for chip in range(CHIPS)] for core in range(2)]


def swap_core(value):
    return lax.ppermute(value, "exp", [(p, p ^ 1) for p in range(OWNERS)])


def swap_across(value):
    return lax.ppermute(value, "exp", [(p, p ^ 2) for p in range(OWNERS)])


def swap_tok(value, partner):
    pairs = [(z * OWNERS + p, partner(z, p % 2) * OWNERS + p) for z in range(DEPTH) for p in range(OWNERS)]
    return lax.ppermute(value, ("tok", "exp"), pairs)


def swap_near(value, step):
    def partner(z, core):
        return (z + 1) % DEPTH if (z + step + core) % 2 == 0 else (z - 1) % DEPTH

    return swap_tok(value, partner)


def near_order(z, core):
    turned = lax.rem(z - core + DEPTH, DEPTH)
    pair, odd = turned // 2, lax.rem(turned, 2)
    away = jnp.where(odd == 1, 1, -1)
    pairs = [pair]
    for step in range(1, DEPTH // 2):
        reach = (step + 1) // 2
        pairs.append(pair + (away * reach if step % 2 else -away * reach))
    chunks = [2 * p + half + core for p in pairs for half in range(2)]
    return odd == 1, lax.rem(jnp.stack(chunks) + 2 * DEPTH, DEPTH).astype(jnp.int32)


def hidden_kernel(order, *refs):
    items, weights, outs = refs[:DEPTH], refs[DEPTH : -BLOCKS], refs[-BLOCKS:]
    depth = items[0].shape[2]
    total = None
    for number in range(DEPTH):
        pair, half = number // 2, number % 2
        left = jnp.concatenate([items[pair][half], items[DEPTH // 2 + pair][half]], axis=0)
        rows = pl.ds(pl.multiple_of(order[number] * depth, depth), depth)
        right = jnp.concatenate([weight[rows, :] for weight in weights], axis=1)
        term = jnp.dot(left, right, preferred_element_type=jnp.float32)
        total = term if total is None else total + term
    units = total.shape[1] // 2
    gate, up = total[:, :units], total[:, units:]
    hidden = (gate / (1.0 + jnp.exp(-gate)) * up).astype(outs[0].dtype)
    for block, out in enumerate(outs):
        out[...] = hidden[block * BLOCK : (block + 1) * BLOCK]


def down_kernel(order, scale, *refs):
    items, weights, out = refs[:DEPTH], refs[DEPTH:-1], refs[-1]
    depth = items[0].shape[2] // len(weights)
    total = None
    for number in range(DEPTH):
        pair, half = number // 2, number % 2
        left = jnp.concatenate([items[pair][half], items[DEPTH // 2 + pair][half]], axis=0)
        rows = pl.ds(pl.multiple_of(order[number] * depth, depth), depth)
        right = jnp.concatenate([weight[rows, :] for weight in weights], axis=0)
        term = jnp.dot(left, right, preferred_element_type=jnp.float32)
        total = term if total is None else total + term
    out[...] = (total * scale[:, :1]).astype(out.dtype)


def kernel_call(kernel, name, order, inner, outs, flops):
    in_vmem = pl.BlockSpec(memory_space=pltpu.VMEM)
    return pl.pallas_call(
        kernel,
        out_shape=[jax.ShapeDtypeStruct(shape, jnp.bfloat16) for shape in outs],
        in_specs=[pl.BlockSpec(memory_space=pltpu.SMEM)] + [in_vmem] * len(inner),
        out_specs=[in_vmem] * len(outs),
        compiler_params=pltpu.CompilerParams(vmem_limit_bytes=20 << 20),
        cost_estimate=pl.CostEstimate(
            flops=flops, bytes_accessed=2 * sum(array.size for array in inner), transcendentals=0
        ),
        name=name,
    )(order, *inner)


def gather_near(chunk, odd):
    other = swap_near(chunk, 0)
    items = [jnp.stack([jnp.where(odd, other, chunk), jnp.where(odd, chunk, other)])]
    for step in range(1, DEPTH // 2):
        items.append(swap_near(items[-1], step))
    return items


def shards(tokens, picked_blocks, gate_scale, w_gate, w_up, w_down):
    position = lax.axis_index("exp")
    z = lax.axis_index("tok")
    core = lax.rem(position, 2)
    share = lax.rem(position, SPAN)
    expert = position // SPAN
    features, units = tokens.shape[1], w_gate.shape[2]
    chosen = lax.dynamic_index_in_dim(picked_blocks, expert, 0, keepdims=False)
    blocks = chosen.shape[0] // SPAN
    rows = blocks * BLOCK
    mine = lax.dynamic_slice_in_dim(chosen, blocks * share, blocks)
    theirs = lax.dynamic_slice_in_dim(chosen, blocks * jnp.bitwise_xor(share, 1), blocks)
    here = (lax.rem(mine, 2) == core)[:, None, None]
    odd, order = near_order(z, core)
    scale = lax.dynamic_index_in_dim(gate_scale, expert, 0, keepdims=False).reshape(SPAN, rows, 1)
    scale = jnp.broadcast_to(lax.dynamic_index_in_dim(scale, share, 0, keepdims=False), (rows, 128))
    names = jnp.concatenate([mine, theirs])
    match = names[None, :] == (2 * jnp.arange(CHIPS, dtype=jnp.int32) + core)[:, None]
    wanted, source = match.any(1)[:, None, None], jnp.argmax(match, 1)

    own = [w_gate[0], w_up[0], w_down[0]]
    spread = jnp.broadcast_to(tokens[None], (CHIPS,) + tokens.shape)
    held = lax.all_to_all(spread, "exp", 0, 0, axis_index_groups=SAME_CORE, tiled=True)
    near = [swap_core(w) for w in own]
    held, sent = lax.optimization_barrier((held, own))
    far = [swap_across(w) for w in sent]
    lent = swap_core(held[theirs // 2])
    selected = jnp.where(here, held[mine // 2], lent)
    selected, near, odd, order, scale, wanted, source = lax.optimization_barrier(
        (selected, near, odd, order, scale, wanted, source)
    )

    chains = [gather_near(selected[block], odd) for block in range(blocks)]
    far_in, _ = lax.optimization_barrier((far[:2], [chain[RELAY] for chain in chains]))
    relayed = [swap_core(w) for w in far_in]
    flops = 2 * rows * DEPTH * features * 2 * SPAN * units
    parts = kernel_call(
        hidden_kernel, "hidden", order,
        [item for chain in chains for item in chain] + [w[kind] for kind in range(2) for w in (own, near, far_in, relayed)],
        [(BLOCK, SPAN * units)] * blocks, flops,
    )

    chains = [gather_near(part, odd) for part in parts]
    far_down, _ = lax.optimization_barrier((far[2], [chain[RELAY // 2] for chain in chains]))
    (done,) = kernel_call(
        down_kernel, "down", order,
        [scale] + [item for chain in chains for item in chain] + [own[2], near[2], far_down, swap_core(far_down)],
        [(rows, features)], flops // 2,
    )
    done = done.reshape(blocks, BLOCK, features)

    all_done = jnp.concatenate([done, swap_core(done)])
    outgoing = jnp.where(wanted, all_done[source], 0)
    arrived = lax.all_to_all(outgoing, "exp", 0, 0, axis_index_groups=SAME_CORE, tiled=True)
    return jnp.sum(arrived, axis=0, dtype=jnp.float32).astype(jnp.bfloat16)


def solution(mesh):
    return jax.shard_map(
        shards,
        mesh=mesh,
        in_specs=(
            P("exp", "tok"),
            P(),
            P(),
            P("exp", None, "tok"),
            P("exp", None, "tok"),
            P("exp", None, "tok"),
        ),
        out_specs=P("exp", "tok"),
        check_vma=False,
    )
```

```python
import jax
import jax.numpy as jnp
from jax import lax
from jax.experimental import pallas as pl
from jax.experimental.pallas import tpu as pltpu
from jax.sharding import PartitionSpec as P

BLOCK = 128
SPAN = 4
CHIPS = 16
DEPTH = 16
OWNERS = 32
BLOCKS = 2
SAME_CORE = [[2 * chip + core for chip in range(CHIPS)] for core in range(2)]


def swap_core(value):
    return lax.ppermute(value, "exp", [(p, p ^ 1) for p in range(OWNERS)])


def swap_across(value):
    return lax.ppermute(value, "exp", [(p, p ^ 2) for p in range(OWNERS)])


def swap_tok(value, partner):
    pairs = [(z * OWNERS + p, partner(z, p % 2) * OWNERS + p) for z in range(DEPTH) for p in range(OWNERS)]
    return lax.ppermute(value, ("tok", "exp"), pairs)


def swap_near(value, step):
    def partner(z, core):
        return (z + 1) % DEPTH if (z + step + core) % 2 == 0 else (z - 1) % DEPTH

    return swap_tok(value, partner)


def near_order(z, core):
    turned = lax.rem(z - core + DEPTH, DEPTH)
    pair, odd = turned // 2, lax.rem(turned, 2)
    away = jnp.where(odd == 1, 1, -1)
    pairs = [pair]
    for step in range(1, DEPTH // 2):
        reach = (step + 1) // 2
        pairs.append(pair + (away * reach if step % 2 else -away * reach))
    chunks = [2 * p + half + core for p in pairs for half in range(2)]
    return odd == 1, lax.rem(jnp.stack(chunks) + 2 * DEPTH, DEPTH).astype(jnp.int32)


def hidden_kernel(gathered, *refs):
    weights, outs = refs[:-BLOCKS], refs[-BLOCKS:]
    depth = gathered.shape[2]
    total = None
    for number in range(DEPTH):
        rows = pl.ds(number * depth, depth)
        right = jnp.concatenate([weight[rows, :] for weight in weights], axis=1)
        term = jnp.dot(gathered[number], right, preferred_element_type=jnp.float32)
        total = term if total is None else total + term
    units = total.shape[1] // 2
    gate, up = total[:, :units], total[:, units:]
    hidden = (gate / (1.0 + jnp.exp(-gate)) * up).astype(outs[0].dtype)
    for block, out in enumerate(outs):
        out[...] = hidden[block * BLOCK : (block + 1) * BLOCK]


def down_kernel(order, scale, *refs):
    items, weights, out = refs[:DEPTH], refs[DEPTH:-1], refs[-1]
    depth = items[0].shape[2] // len(weights)
    total = None
    for number in range(DEPTH):
        pair, half = number // 2, number % 2
        left = jnp.concatenate([items[pair][half], items[DEPTH // 2 + pair][half]], axis=0)
        rows = pl.ds(pl.multiple_of(order[number] * depth, depth), depth)
        right = jnp.concatenate([weight[rows, :] for weight in weights], axis=0)
        term = jnp.dot(left, right, preferred_element_type=jnp.float32)
        total = term if total is None else total + term
    out[...] = (total * scale[:, :1]).astype(out.dtype)


def kernel_call(kernel, name, orders, inner, outs, flops):
    in_vmem = pl.BlockSpec(memory_space=pltpu.VMEM)
    return pl.pallas_call(
        kernel,
        out_shape=[jax.ShapeDtypeStruct(shape, jnp.bfloat16) for shape in outs],
        in_specs=[pl.BlockSpec(memory_space=pltpu.SMEM)] * len(orders) + [in_vmem] * len(inner),
        out_specs=[in_vmem] * len(outs),
        compiler_params=pltpu.CompilerParams(vmem_limit_bytes=20 << 20),
        cost_estimate=pl.CostEstimate(
            flops=flops, bytes_accessed=2 * sum(array.size for array in inner), transcendentals=0
        ),
        name=name,
    )(*orders, *inner)


def gather_near(chunk, odd):
    other = swap_near(chunk, 0)
    items = [jnp.stack([jnp.where(odd, other, chunk), jnp.where(odd, chunk, other)])]
    for step in range(1, DEPTH // 2):
        items.append(swap_near(items[-1], step))
    return items


def shards(tokens, picked_blocks, gate_scale, w_gate, w_up, w_down):
    position = lax.axis_index("exp")
    z = lax.axis_index("tok")
    core = lax.rem(position, 2)
    share = lax.rem(position, SPAN)
    expert = position // SPAN
    features, units = tokens.shape[1], w_gate.shape[2]
    chosen = lax.dynamic_index_in_dim(picked_blocks, expert, 0, keepdims=False)
    blocks = chosen.shape[0] // SPAN
    rows = blocks * BLOCK
    mine = lax.dynamic_slice_in_dim(chosen, blocks * share, blocks)
    theirs = lax.dynamic_slice_in_dim(chosen, blocks * jnp.bitwise_xor(share, 1), blocks)
    here = (lax.rem(mine, 2) == core)[:, None, None]
    odd, order = near_order(z, core)
    scale = lax.dynamic_index_in_dim(gate_scale, expert, 0, keepdims=False).reshape(SPAN, rows, 1)
    scale = jnp.broadcast_to(lax.dynamic_index_in_dim(scale, share, 0, keepdims=False), (rows, 128))
    names = jnp.concatenate([mine, theirs])
    match = names[None, :] == (2 * jnp.arange(CHIPS, dtype=jnp.int32) + core)[:, None]
    wanted, source = match.any(1)[:, None, None], jnp.argmax(match, 1)

    own = [w_gate[0], w_up[0], w_down[0]]
    spread = jnp.broadcast_to(tokens[None], (CHIPS,) + tokens.shape)
    held = lax.all_to_all(spread, "exp", 0, 0, axis_index_groups=SAME_CORE, tiled=True)
    near = [swap_core(w) for w in own]
    held, sent = lax.optimization_barrier((held, own))
    far = [swap_across(w) for w in sent]
    lent = swap_core(held[theirs // 2])
    selected = jnp.where(here, held[mine // 2], lent)
    selected, near, odd, order, scale, wanted, source = lax.optimization_barrier(
        (selected, near, odd, order, scale, wanted, source)
    )

    gathered = lax.all_gather(selected.reshape(rows, features), "tok")
    relayed = [swap_core(w) for w in far]
    gathered, relayed = lax.optimization_barrier((gathered, relayed))
    flops = 2 * rows * DEPTH * features * 2 * SPAN * units
    parts = kernel_call(
        hidden_kernel, "hidden", [],
        [gathered] + [w[kind] for kind in range(2) for w in (own, near, far, relayed)],
        [(BLOCK, SPAN * units)] * blocks, flops,
    )

    chains = [gather_near(part, odd) for part in parts]
    (done,) = kernel_call(
        down_kernel, "down", [order],
        [scale] + [item for chain in chains for item in chain] + [w[2] for w in (own, near, far, relayed)],
        [(rows, features)], flops // 2,
    )
    done = done.reshape(blocks, BLOCK, features)

    all_done = jnp.concatenate([done, swap_core(done)])
    outgoing = jnp.where(wanted, all_done[source], 0)
    arrived = lax.all_to_all(outgoing, "exp", 0, 0, axis_index_groups=SAME_CORE, tiled=True)
    return jnp.sum(arrived, axis=0, dtype=jnp.float32).astype(jnp.bfloat16)


def solution(mesh):
    return jax.shard_map(
        shards,
        mesh=mesh,
        in_specs=(
            P("exp", "tok"),
            P(),
            P(),
            P("exp", None, "tok"),
            P("exp", None, "tok"),
            P("exp", None, "tok"),
        ),
        out_specs=P("exp", "tok"),
        check_vma=False,
    )
```

```python
import jax
import jax.numpy as jnp
from jax import lax
from jax.experimental import pallas as pl
from jax.experimental.pallas import tpu as pltpu
from jax.sharding import PartitionSpec as P

BLOCK = 128
SPAN = 4
CHIPS = 16
DEPTH = 16
OWNERS = 32
SAME_CORE = [[2 * chip + core for chip in range(CHIPS)] for core in range(2)]
TAIL = 8
TOP = 14.0


def swap_core(value):
    return lax.ppermute(value, "exp", [(p, p ^ 1) for p in range(OWNERS)])


def encode(value):
    value = value.astype(jnp.float32)
    largest = jnp.maximum(jnp.max(jnp.abs(value)), 1e-30)
    exponent = jnp.ceil(jnp.log2(largest))
    scaled = (value * jnp.exp2(TOP - exponent)).astype(jnp.float16)
    tail = jnp.full((TAIL, value.shape[1]), exponent, jnp.float16)
    return jnp.concatenate([scaled, tail])


def decode(coded):
    exponent = coded[..., -TAIL:, :][..., :1, :1].astype(jnp.float32)
    value = coded[..., :-TAIL, :].astype(jnp.float32) * jnp.exp2(exponent - TOP)
    return value.astype(jnp.bfloat16)


def hidden_kernel(gathered, *refs):
    weights, out = refs[:-1], refs[-1]
    depth = gathered.shape[2]
    total = None
    for number in range(DEPTH):
        rows = pl.ds(number * depth, depth)
        right = jnp.concatenate([weight[rows, :] for weight in weights], axis=1)
        term = jnp.dot(gathered[number], right, preferred_element_type=jnp.float32)
        total = term if total is None else total + term
    units = total.shape[1] // 2
    gate, up = total[:, :units], total[:, units:]
    out[...] = (gate / (1.0 + jnp.exp(-gate)) * up).astype(out.dtype)


def down_kernel(gathered, scale, *refs):
    weights, out = refs[:-1], refs[-1]
    depth = gathered.shape[2] // len(weights)
    total = None
    for number in range(DEPTH):
        rows = pl.ds(number * depth, depth)
        right = jnp.concatenate([weight[rows, :] for weight in weights], axis=0)
        term = jnp.dot(gathered[number], right, preferred_element_type=jnp.float32)
        total = term if total is None else total + term
    out[...] = (total * scale[:, :1]).astype(out.dtype)


def kernel_call(kernel, name, inner, rows, columns, flops):
    in_vmem = pl.BlockSpec(memory_space=pltpu.VMEM)
    return pl.pallas_call(
        kernel,
        out_shape=jax.ShapeDtypeStruct((rows, columns), jnp.bfloat16),
        in_specs=[in_vmem] * len(inner),
        out_specs=in_vmem,
        compiler_params=pltpu.CompilerParams(vmem_limit_bytes=24 << 20),
        cost_estimate=pl.CostEstimate(
            flops=flops, bytes_accessed=2 * sum(array.size for array in inner), transcendentals=0
        ),
        name=name,
    )(*inner)


def shards(tokens, picked_blocks, gate_scale, w_gate, w_up, w_down):
    position = lax.axis_index("exp")
    core = lax.rem(position, 2)
    expert = position // SPAN
    features, units = tokens.shape[1], w_gate.shape[2]
    chosen = lax.dynamic_index_in_dim(picked_blocks, expert, 0, keepdims=False)
    half = chosen.shape[0] // 2
    rows = half * BLOCK
    mine = lax.dynamic_slice_in_dim(chosen, half * core, half)
    theirs = lax.dynamic_slice_in_dim(chosen, half * (1 - core), half)
    scale = lax.dynamic_index_in_dim(gate_scale, expert, 0, keepdims=False).reshape(2, rows, 1)
    scale = jnp.broadcast_to(lax.dynamic_index_in_dim(scale, core, 0, keepdims=False), (rows, 128))
    names = jnp.concatenate([mine, theirs])
    match = names[None, :] == (2 * jnp.arange(CHIPS, dtype=jnp.int32) + core)[:, None]
    wanted, source = match.any(1)[:, None, None], jnp.argmax(match, 1)

    own = [w_gate[0], w_up[0], w_down[0]]
    near = [swap_core(w) for w in own]

    coded = encode(tokens)
    coded, scale, wanted, source, mine = lax.optimization_barrier((coded, scale, wanted, source, mine))
    held = lax.all_gather(coded, "exp")
    picked = jnp.stack([lax.dynamic_index_in_dim(held, mine[pick], 0, keepdims=False) for pick in range(half)])
    gathered = decode(lax.all_gather(picked, "tok")).reshape(DEPTH, rows, features)
    flops = 2 * rows * DEPTH * features * 4 * units
    hidden = kernel_call(
        hidden_kernel, "hidden", [gathered] + [w[kind] for kind in range(2) for w in (own, near)], rows, 2 * units, flops
    )
    gathered = decode(lax.all_gather(encode(hidden)[None], "tok", tiled=True))
    done = kernel_call(
        down_kernel, "down", [gathered, scale] + [w[2] for w in (own, near)], rows, features, flops // 2
    )
    done = done.reshape(half, BLOCK, features)

    all_done = jnp.concatenate([done, swap_core(done)])
    outgoing = jnp.where(wanted, all_done[source], 0)
    arrived = lax.all_to_all(outgoing, "exp", 0, 0, axis_index_groups=SAME_CORE, tiled=True)
    return jnp.sum(arrived, axis=0, dtype=jnp.float32).astype(jnp.bfloat16)


def solution(mesh):
    return jax.shard_map(
        shards,
        mesh=mesh,
        in_specs=(
            P("exp", "tok"),
            P(),
            P(),
            P("exp", None, "tok"),
            P("exp", None, "tok"),
            P("exp", None, "tok"),
        ),
        out_specs=P("exp", "tok"),
        check_vma=False,
    )
```

```python
import jax
import jax.numpy as jnp
from jax import lax
from jax.experimental import pallas as pl
from jax.experimental.pallas import tpu as pltpu
from jax.sharding import PartitionSpec as P

BLOCK = 128
SPAN = 4
CHIPS = 16
DEPTH = 16
OWNERS = 32
SAME_CORE = [[2 * chip + core for chip in range(CHIPS)] for core in range(2)]
TAIL = 8
TOP = 14.0
CORE, EXPERT = 8, 9


def swap_core(value):
    return lax.ppermute(value, "exp", [(p, p ^ 1) for p in range(OWNERS)])


def encode(value):
    value = value.astype(jnp.float32)
    largest = jnp.maximum(jnp.max(jnp.abs(value)), 1e-30)
    exponent = jnp.ceil(jnp.log2(largest))
    scaled = (value * jnp.exp2(TOP - exponent)).astype(jnp.float16)
    tail = jnp.full((TAIL, value.shape[1]), exponent, jnp.float16)
    return jnp.concatenate([scaled, tail])


def decode(coded):
    exponent = jnp.max(coded[..., -TAIL:, :], axis=(-2, -1), keepdims=True).astype(jnp.float32)
    value = coded[..., :-TAIL, :].astype(jnp.float32) * jnp.exp2(exponent - TOP)
    return value.astype(jnp.bfloat16)


def hidden_kernel(facts, gathered, *refs):
    weights, out = refs[:-1], refs[-1]
    depth = gathered.shape[2]
    total = None
    for number in range(DEPTH):
        rows = pl.ds(number * depth, depth)
        right = jnp.concatenate([weight[rows, :] for weight in weights], axis=1)
        term = jnp.dot(gathered[number], right, preferred_element_type=jnp.float32)
        total = term if total is None else total + term
    units = total.shape[1] // 2
    gate, up = total[:, :units], total[:, units:]
    out[...] = (gate / (1.0 + jnp.exp(-gate)) * up).astype(out.dtype)


def down_kernel(facts, gathered, scales, *refs):
    weights, out = refs[:-1], refs[-1]
    depth = gathered.shape[2] // len(weights)
    total = None
    for number in range(DEPTH):
        rows = pl.ds(number * depth, depth)
        right = jnp.concatenate([weight[rows, :] for weight in weights], axis=0)
        term = jnp.dot(gathered[number], right, preferred_element_type=jnp.float32)
        total = term if total is None else total + term
    count = total.shape[0]
    both = scales[pl.ds(facts[EXPERT], 1), :]
    scale = jnp.where(facts[CORE] == 0, both[:, :count], both[:, count:])
    scale = jnp.broadcast_to(scale, (128, count)).T
    out[...] = (total * scale[:, :1]).astype(out.dtype)


def place_kernel(facts, done, others, out):
    out[...] = jnp.zeros_like(out)
    count = done.shape[0]
    for pick in range(2 * count):
        block = facts[pick]
        source = done if pick < count else others

        @pl.when(lax.rem(block, 2) == facts[CORE])
        def _():
            out[pl.ds(lax.div(block, 2), 1)] = source[pl.ds(pick % count, 1)]


def kernel_call(kernel, name, facts, inner, shape, flops):
    in_vmem = pl.BlockSpec(memory_space=pltpu.VMEM)
    return pl.pallas_call(
        kernel,
        out_shape=jax.ShapeDtypeStruct(shape, jnp.bfloat16),
        in_specs=[pl.BlockSpec(memory_space=pltpu.SMEM)] + [in_vmem] * len(inner),
        out_specs=in_vmem,
        compiler_params=pltpu.CompilerParams(vmem_limit_bytes=24 << 20),
        cost_estimate=pl.CostEstimate(
            flops=flops, bytes_accessed=2 * sum(array.size for array in inner), transcendentals=0
        ),
        name=name,
    )(facts, *inner)


def shards(tokens, picked_blocks, gate_scale, w_gate, w_up, w_down):
    position = lax.axis_index("exp")
    core = lax.rem(position, 2)
    expert = position // SPAN
    features, units = tokens.shape[1], w_gate.shape[2]
    chosen = lax.dynamic_index_in_dim(picked_blocks, expert, 0, keepdims=False)
    half = chosen.shape[0] // 2
    rows = half * BLOCK
    mine = lax.dynamic_slice_in_dim(chosen, half * core, half)
    theirs = lax.dynamic_slice_in_dim(chosen, half * (1 - core), half)
    facts = jnp.concatenate([mine, theirs, jnp.stack([core, expert]).astype(jnp.int32)])

    own = [w_gate[0], w_up[0], w_down[0]]
    near = [swap_core(w) for w in own]

    coded, facts, mine = lax.optimization_barrier((encode(tokens), facts, mine))
    held = lax.all_gather(coded, "exp")
    gathered = decode(lax.all_gather(held[mine], "tok")).reshape(DEPTH, rows, features)
    flops = 2 * rows * DEPTH * features * 4 * units
    hidden = kernel_call(
        hidden_kernel, "hidden", facts, [gathered] + [w[kind] for kind in range(2) for w in (own, near)],
        (rows, 2 * units), flops,
    )
    gathered = decode(lax.all_gather(encode(hidden)[None], "tok", tiled=True))
    done = kernel_call(
        down_kernel, "down", facts, [gathered, gate_scale] + [w[2] for w in (own, near)], (rows, features), flops // 2
    ).reshape(half, BLOCK, features)

    outgoing = kernel_call(place_kernel, "place", facts, [done, swap_core(done)], (CHIPS, BLOCK, features), 0)
    arrived = lax.all_to_all(outgoing, "exp", 0, 0, axis_index_groups=SAME_CORE, tiled=True)
    return jnp.sum(arrived, axis=0, dtype=jnp.float32).astype(jnp.bfloat16)


def solution(mesh):
    return jax.shard_map(
        shards,
        mesh=mesh,
        in_specs=(
            P("exp", "tok"),
            P(),
            P(),
            P("exp", None, "tok"),
            P("exp", None, "tok"),
            P("exp", None, "tok"),
        ),
        out_specs=P("exp", "tok"),
        check_vma=False,
    )
```

```python
import jax
import jax.numpy as jnp
from jax import lax
from jax.experimental import pallas as pl
from jax.experimental.pallas import tpu as pltpu
from jax.sharding import PartitionSpec as P

BLOCK = 128
SPAN = 4
CHIPS = 16
DEPTH = 16
OWNERS = 32
SAME_CORE = [[2 * chip + core for chip in range(CHIPS)] for core in range(2)]
TAIL = 8
TOP = 14.0
CORE, EXPERT, SHARE = 4, 5, 6


def swap_across(value):
    return lax.ppermute(value, "exp", [(p, p ^ 2) for p in range(OWNERS)])


def swap_core(value):
    return lax.ppermute(value, "exp", [(p, p ^ 1) for p in range(OWNERS)])


def encode(value, largest):
    exponent = jnp.ceil(jnp.log2(jnp.maximum(largest, 1e-30)))
    scaled = (value.astype(jnp.float32) * jnp.exp2(TOP - exponent)).astype(jnp.float16)
    tail = jnp.broadcast_to(exponent.astype(jnp.float16), (TAIL, value.shape[1]))
    return jnp.concatenate([scaled, tail])


def decode(coded):
    exponent = jnp.max(coded[..., -TAIL:, :], axis=-2, keepdims=True).astype(jnp.float32)
    value = coded[..., :-TAIL, :].astype(jnp.float32) * jnp.exp2(exponent - TOP)
    return value.astype(jnp.bfloat16)


def hidden_kernel(facts, gathered, *refs):
    weights, (out, largest) = refs[:-2], refs[-2:]
    depth = gathered.shape[2]
    total = None
    for number in range(DEPTH):
        rows = pl.ds(number * depth, depth)
        right = jnp.concatenate([weight[kind, rows, :] for kind in range(2) for weight in weights], axis=1)
        term = jnp.dot(gathered[number], right, preferred_element_type=jnp.float32)
        total = term if total is None else total + term
    units = total.shape[1] // 2
    gate, up = total[:, :units], total[:, units:]
    hidden = gate / (1.0 + jnp.exp(-gate)) * up
    out[...] = hidden.astype(out.dtype)
    largest[...] = jnp.max(jnp.abs(hidden), axis=0, keepdims=True)


def down_kernel(facts, gathered, scales, *refs):
    weights, out = refs[:-1], refs[-1]
    depth = gathered.shape[2] // len(weights)
    total = None
    for number in range(DEPTH):
        rows = pl.ds(number * depth, depth)
        right = jnp.concatenate([weight[rows, :] for weight in weights], axis=0)
        term = jnp.dot(gathered[number], right, preferred_element_type=jnp.float32)
        total = term if total is None else total + term
    count = total.shape[0]
    columns = pl.ds(pl.multiple_of(facts[SHARE] * count, count), count)
    scale = scales[pl.ds(facts[EXPERT], 1), columns]
    scale = jnp.broadcast_to(scale, (128, count)).T
    out[...] = (total * scale[:, :1]).astype(out.dtype)


def place_kernel(facts, done, others, out):
    out[...] = jnp.zeros_like(out)
    count = done.shape[0]
    for pick in range(2 * count):
        block = facts[pick]
        source = done if pick < count else others

        @pl.when(lax.rem(block, 2) == facts[CORE])
        def _():
            out[pl.ds(lax.div(block, 2), 1)] = source[pl.ds(pick % count, 1)]


def array_of(*shape):
    return jax.ShapeDtypeStruct(shape, jnp.bfloat16)


def kernel_call(kernel, name, facts, inner, outs, flops):
    in_vmem = pl.BlockSpec(memory_space=pltpu.VMEM)
    return pl.pallas_call(
        kernel,
        out_shape=outs,
        in_specs=[pl.BlockSpec(memory_space=pltpu.SMEM)] + [in_vmem] * len(inner),
        out_specs=[in_vmem] * len(outs),
        compiler_params=pltpu.CompilerParams(vmem_limit_bytes=24 << 20),
        cost_estimate=pl.CostEstimate(
            flops=flops, bytes_accessed=2 * sum(array.size for array in inner), transcendentals=0
        ),
        name=name,
    )(facts, *inner)


def shards(tokens, picked_blocks, gate_scale, w_gate, w_up, w_down):
    position = lax.axis_index("exp")
    core = lax.rem(position, 2)
    expert = position // SPAN
    features, units = tokens.shape[1], w_gate.shape[2]
    chosen = lax.dynamic_index_in_dim(picked_blocks, expert, 0, keepdims=False)
    share = lax.rem(position, SPAN)
    blocks = chosen.shape[0] // SPAN
    rows = blocks * BLOCK
    mine = lax.dynamic_slice_in_dim(chosen, blocks * share, blocks)
    theirs = lax.dynamic_slice_in_dim(chosen, blocks * jnp.bitwise_xor(share, 1), blocks)
    facts = jnp.concatenate([mine, theirs, jnp.stack([core, expert, share]).astype(jnp.int32)])

    in_own, down_own = jnp.stack([w_gate[0], w_up[0]]), w_down[0]
    in_near, down_near = swap_core(in_own), swap_core(down_own)
    largest = jnp.max(jnp.abs(tokens.astype(jnp.float32)), axis=0, keepdims=True)
    coded, facts, mine = lax.optimization_barrier((encode(tokens, largest), facts, mine))
    held = lax.all_gather(coded, "exp")
    held, in_sent, down_sent = lax.optimization_barrier((held, in_own, down_own))
    in_far, down_far = swap_across(in_sent), swap_across(down_sent)
    gathered = lax.all_gather(held[mine], "tok")
    gathered, in_far = lax.optimization_barrier((gathered, in_far))
    in_last = swap_core(in_far)
    flops = 2 * rows * DEPTH * features * 2 * SPAN * units
    hidden, largest = kernel_call(
        hidden_kernel, "hidden", facts,
        [decode(gathered).reshape(DEPTH, rows, features), in_own, in_near, in_far, in_last],
        [array_of(rows, SPAN * units), jax.ShapeDtypeStruct((1, SPAN * units), jnp.float32)], flops,
    )
    gathered = lax.all_gather(encode(hidden, largest)[None], "tok", tiled=True)
    gathered, down_far = lax.optimization_barrier((gathered, down_far))
    down_last = swap_core(down_far)
    (done,) = kernel_call(
        down_kernel, "down", facts, [decode(gathered), gate_scale, down_own, down_near, down_far, down_last],
        [array_of(rows, features)], flops // 2,
    )
    done = done.reshape(blocks, BLOCK, features)

    (outgoing,) = kernel_call(
        place_kernel, "place", facts, [done, swap_core(done)], [array_of(CHIPS, BLOCK, features)], 0
    )
    arrived = lax.all_to_all(outgoing, "exp", 0, 0, axis_index_groups=SAME_CORE, tiled=True)
    return jnp.sum(arrived, axis=0, dtype=jnp.float32).astype(jnp.bfloat16)


def solution(mesh):
    return jax.shard_map(
        shards,
        mesh=mesh,
        in_specs=(
            P("exp", "tok"),
            P(),
            P(),
            P("exp", None, "tok"),
            P("exp", None, "tok"),
            P("exp", None, "tok"),
        ),
        out_specs=P("exp", "tok"),
        check_vma=False,
    )
```

```python
import jax
import jax.numpy as jnp
from jax import lax
from jax.experimental import pallas as pl
from jax.experimental.pallas import tpu as pltpu
from jax.sharding import PartitionSpec as P

BLOCK = 128
SPAN = 4
CHIPS = 16
DEPTH = 16
OWNERS = 32
SAME_CORE = [[2 * chip + core for chip in range(CHIPS)] for core in range(2)]
TAIL = 8
TOP = 14.0
CORE, EXPERT, SHARE = 4, 5, 6


def swap_across(value):
    return lax.ppermute(value, "exp", [(p, p ^ 2) for p in range(OWNERS)])


def swap_core(value):
    return lax.ppermute(value, "exp", [(p, p ^ 1) for p in range(OWNERS)])


def encode(value, largest):
    exponent = jnp.ceil(jnp.log2(jnp.maximum(largest, 1e-30)))
    scaled = (value.astype(jnp.float32) * jnp.exp2(TOP - exponent)).astype(jnp.float16)
    tail = jnp.broadcast_to(exponent.astype(jnp.float16), (TAIL, value.shape[1]))
    return jnp.concatenate([scaled, tail])


def decode(coded):
    exponent = jnp.max(coded[..., -TAIL:, :], axis=-2, keepdims=True).astype(jnp.float32)
    value = coded[..., :-TAIL, :].astype(jnp.float32) * jnp.exp2(exponent - TOP)
    return value.astype(jnp.bfloat16)


def hidden_kernel(facts, gathered, *refs):
    weights, (out, largest) = refs[:-2], refs[-2:]
    depth = gathered.shape[2]
    total = None
    for number in range(DEPTH):
        rows = pl.ds(number * depth, depth)
        right = jnp.concatenate([weight[kind, rows, :] for kind in range(2) for weight in weights], axis=1)
        term = jnp.dot(gathered[number], right, preferred_element_type=jnp.float32)
        total = term if total is None else total + term
    units = total.shape[1] // 2
    gate, up = total[:, :units], total[:, units:]
    hidden = gate / (1.0 + jnp.exp(-gate)) * up
    out[...] = hidden.astype(out.dtype)
    largest[...] = jnp.max(jnp.abs(hidden), axis=0, keepdims=True)


def down_kernel(facts, gathered, scales, *refs):
    weights, (kept, given) = refs[:-2], refs[-2:]
    depth = gathered.shape[2] // len(weights)
    total = None
    for number in range(DEPTH):
        rows = pl.ds(number * depth, depth)
        right = jnp.concatenate([weight[rows, :] for weight in weights], axis=0)
        term = jnp.dot(gathered[number], right, preferred_element_type=jnp.float32)
        total = term if total is None else total + term
    count = total.shape[0] // 2
    parts = []
    for share in (facts[SHARE], facts[SHARE] + 1 - 2 * facts[CORE]):
        columns = pl.ds(pl.multiple_of(share * count, count), count)
        parts.append(scales[pl.ds(facts[EXPERT], 1), columns])
    scale = jnp.broadcast_to(jnp.concatenate(parts, axis=1), (128, 2 * count)).T
    total = total * scale[:, :1]
    kept[...] = total
    given[...] = total.astype(given.dtype)


def place_kernel(facts, kept, taken, out):
    out[...] = jnp.zeros_like(out)
    count = kept.shape[0]
    for pick in range(count):
        block = facts[pick]

        @pl.when(lax.rem(block, 2) == facts[CORE])
        def _():
            both = kept[pick] + taken[(pick + count // 2) % count].astype(jnp.float32)
            out[pl.ds(lax.div(block, 2), 1)] = both.astype(out.dtype)[None]


def array_of(*shape):
    return jax.ShapeDtypeStruct(shape, jnp.bfloat16)


def kernel_call(kernel, name, facts, inner, outs, flops):
    in_vmem = pl.BlockSpec(memory_space=pltpu.VMEM)
    return pl.pallas_call(
        kernel,
        out_shape=outs,
        in_specs=[pl.BlockSpec(memory_space=pltpu.SMEM)] + [in_vmem] * len(inner),
        out_specs=[in_vmem] * len(outs),
        compiler_params=pltpu.CompilerParams(vmem_limit_bytes=24 << 20),
        cost_estimate=pl.CostEstimate(
            flops=flops, bytes_accessed=2 * sum(array.size for array in inner), transcendentals=0
        ),
        name=name,
    )(facts, *inner)


def shards(tokens, picked_blocks, gate_scale, w_gate, w_up, w_down):
    position = lax.axis_index("exp")
    core = lax.rem(position, 2)
    expert = position // SPAN
    features, units = tokens.shape[1], w_gate.shape[2]
    chosen = lax.dynamic_index_in_dim(picked_blocks, expert, 0, keepdims=False)
    share = lax.rem(position, SPAN)
    blocks = chosen.shape[0] // SPAN
    rows = blocks * BLOCK
    mine = lax.dynamic_slice_in_dim(chosen, blocks * share, blocks)
    theirs = lax.dynamic_slice_in_dim(chosen, blocks * jnp.bitwise_xor(share, 1), blocks)
    facts = jnp.concatenate([mine, theirs, jnp.stack([core, expert, share]).astype(jnp.int32)])

    in_own, down_own = jnp.stack([w_gate[0], w_up[0]]), w_down[0]
    largest = jnp.max(jnp.abs(tokens.astype(jnp.float32)), axis=0, keepdims=True)
    coded, facts, mine = lax.optimization_barrier((encode(tokens, largest), facts, mine))
    held = lax.all_gather(coded, "exp")
    held, in_sent, down_sent = lax.optimization_barrier((held, in_own, down_own))
    in_far, down_far = swap_across(in_sent), swap_across(down_sent)
    gathered, in_far = lax.optimization_barrier((lax.all_gather(held[mine], "tok"), in_far))
    gathered = decode(jnp.concatenate([gathered, swap_core(gathered)], axis=1)).reshape(DEPTH, 2 * rows, features)
    flops = 4 * rows * DEPTH * features * SPAN * units
    hidden, largest = kernel_call(
        hidden_kernel, "hidden", facts, [gathered, in_own, in_far],
        [array_of(2 * rows, 2 * units), jax.ShapeDtypeStruct((1, 2 * units), jnp.float32)], flops,
    )
    gathered = lax.all_gather(encode(hidden, largest)[None], "tok", tiled=True)
    kept, given = kernel_call(
        down_kernel, "down", facts, [decode(gathered), gate_scale, down_own, down_far],
        [jax.ShapeDtypeStruct((2 * rows, features), jnp.float32), array_of(2 * rows, features)], flops // 2,
    )

    whole = (2 * blocks, BLOCK, features)
    (outgoing,) = kernel_call(
        place_kernel, "place", facts, [kept.reshape(whole), swap_core(given).reshape(whole)],
        [array_of(CHIPS, BLOCK, features)], 0,
    )
    arrived = lax.all_to_all(outgoing, "exp", 0, 0, axis_index_groups=SAME_CORE, tiled=True)
    return jnp.sum(arrived, axis=0, dtype=jnp.float32).astype(jnp.bfloat16)


def solution(mesh):
    return jax.shard_map(
        shards,
        mesh=mesh,
        in_specs=(
            P("exp", "tok"),
            P(),
            P(),
            P("exp", None, "tok"),
            P("exp", None, "tok"),
            P("exp", None, "tok"),
        ),
        out_specs=P("exp", "tok"),
        check_vma=False,
    )
```

```python
import jax
import jax.numpy as jnp
from jax import lax
from jax.experimental import pallas as pl
from jax.experimental.pallas import tpu as pltpu
from jax.sharding import PartitionSpec as P

BLOCK = 128
SPAN = 4
CHIPS = 16
DEPTH = 16
OWNERS = 32
LINES = [[z * OWNERS + 2 * chip + core for z in range(DEPTH) for core in range(2)] for chip in range(CHIPS)]
SAME_CORE = [[2 * chip + core for chip in range(CHIPS)] for core in range(2)]
TAIL = 8
TOP = 14.0
CORE, EXPERT, HALF = 4, 5, 6


def swap_across(value):
    return lax.ppermute(value, "exp", [(p, p ^ 2) for p in range(OWNERS)])


def swap_core(value):
    return lax.ppermute(value, "exp", [(p, p ^ 1) for p in range(OWNERS)])


def encode(value, largest):
    exponent = jnp.ceil(jnp.log2(jnp.maximum(largest, 1e-30)))
    scaled = (value.astype(jnp.float32) * jnp.exp2(TOP - exponent)).astype(jnp.float16)
    tail = jnp.broadcast_to(exponent.astype(jnp.float16), (TAIL, value.shape[1]))
    return jnp.concatenate([scaled, tail])


def decode(coded):
    exponent = jnp.max(coded[..., -TAIL:, :], axis=-2, keepdims=True).astype(jnp.float32)
    value = coded[..., :-TAIL, :].astype(jnp.float32) * jnp.exp2(exponent - TOP)
    return value.astype(jnp.bfloat16)


def hidden_kernel(facts, gathered, *refs):
    weights, (out, largest) = refs[:-2], refs[-2:]
    depth = gathered.shape[2]
    total = None
    for number in range(DEPTH):
        rows = pl.ds(number * depth, depth)
        right = jnp.concatenate([weight[kind, rows, :] for kind in range(2) for weight in weights], axis=1)
        term = jnp.dot(gathered[number], right, preferred_element_type=jnp.float32)
        total = term if total is None else total + term
    units = total.shape[1] // 2
    gate, up = total[:, :units], total[:, units:]
    hidden = gate / (1.0 + jnp.exp(-gate)) * up
    out[...] = hidden.astype(out.dtype)
    largest[...] = jnp.max(jnp.abs(hidden), axis=0, keepdims=True)


def down_kernel(facts, gathered, scales, *refs):
    weights, (kept, given) = refs[:-2], refs[-2:]
    depth = gathered.shape[2] // len(weights)
    total = None
    for number in range(DEPTH):
        rows = pl.ds(number * depth, depth)
        right = jnp.concatenate([weight[rows, :] for weight in weights], axis=0)
        term = jnp.dot(gathered[number], right, preferred_element_type=jnp.float32)
        total = term if total is None else total + term
    count = total.shape[0]
    columns = pl.ds(pl.multiple_of(facts[HALF] * count, count), count)
    scale = jnp.broadcast_to(scales[pl.ds(facts[EXPERT], 1), columns], (128, count)).T
    total = total * scale[:, :1]
    kept[...] = total
    given[...] = total.astype(given.dtype)


def place_kernel(facts, kept, taken, out):
    out[...] = jnp.zeros_like(out)
    count = kept.shape[0]
    for pick in range(count):
        block = facts[pick]

        @pl.when(lax.rem(block, 2) == facts[CORE])
        def _():
            both = kept[pick] + taken[pick].astype(jnp.float32)
            out[pl.ds(lax.div(block, 2), 1)] = both.astype(out.dtype)[None]


def array_of(*shape):
    return jax.ShapeDtypeStruct(shape, jnp.bfloat16)


def kernel_call(kernel, name, facts, inner, outs, flops):
    in_vmem = pl.BlockSpec(memory_space=pltpu.VMEM)
    return pl.pallas_call(
        kernel,
        out_shape=outs,
        in_specs=[pl.BlockSpec(memory_space=pltpu.SMEM)] + [in_vmem] * len(inner),
        out_specs=[in_vmem] * len(outs),
        compiler_params=pltpu.CompilerParams(vmem_limit_bytes=24 << 20),
        cost_estimate=pl.CostEstimate(
            flops=flops, bytes_accessed=2 * sum(array.size for array in inner), transcendentals=0
        ),
        name=name,
    )(facts, *inner)


def shards(tokens, picked_blocks, gate_scale, w_gate, w_up, w_down):
    position = lax.axis_index("exp")
    core = lax.rem(position, 2)
    expert = position // SPAN
    features, units = tokens.shape[1], w_gate.shape[2]
    chosen = lax.dynamic_index_in_dim(picked_blocks, expert, 0, keepdims=False)
    side = lax.rem(position, SPAN) // 2
    half = chosen.shape[0] // 2
    rows = half * BLOCK
    picks = lax.dynamic_slice_in_dim(chosen, half * side, half)
    mine = lax.dynamic_slice_in_dim(picks, half // 2 * core, half // 2)
    facts = jnp.concatenate([picks, jnp.stack([core, expert, side]).astype(jnp.int32)])

    in_own, down_own = jnp.stack([w_gate[0], w_up[0]]), w_down[0]
    largest = jnp.max(jnp.abs(tokens.astype(jnp.float32)), axis=0, keepdims=True)
    coded, facts, mine = lax.optimization_barrier((encode(tokens, largest), facts, mine))
    held = lax.all_gather(coded, "exp")
    held, in_sent, down_sent = lax.optimization_barrier((held, in_own, down_own))
    in_far, down_far = swap_across(in_sent), swap_across(down_sent)
    gathered = lax.all_gather(held[mine], ("tok", "exp"), axis_index_groups=LINES)
    gathered, in_far = lax.optimization_barrier((gathered, in_far))
    gathered = decode(gathered).reshape(DEPTH, rows, features)
    flops = 2 * rows * DEPTH * features * SPAN * units
    hidden, largest = kernel_call(
        hidden_kernel, "hidden", facts, [gathered, in_own, in_far],
        [array_of(rows, 2 * units), jax.ShapeDtypeStruct((1, 2 * units), jnp.float32)], flops,
    )
    gathered = lax.all_gather(encode(hidden, largest)[None], "tok", tiled=True)
    kept, given = kernel_call(
        down_kernel, "down", facts, [decode(gathered), gate_scale, down_own, down_far],
        [jax.ShapeDtypeStruct((rows, features), jnp.float32), array_of(rows, features)], flops // 2,
    )

    whole = (half, BLOCK, features)
    (outgoing,) = kernel_call(
        place_kernel, "place", facts, [kept.reshape(whole), swap_core(given).reshape(whole)],
        [array_of(CHIPS, BLOCK, features)], 0,
    )
    arrived = lax.all_to_all(outgoing, "exp", 0, 0, axis_index_groups=SAME_CORE, tiled=True)
    return jnp.sum(arrived, axis=0, dtype=jnp.float32).astype(jnp.bfloat16)


def solution(mesh):
    return jax.shard_map(
        shards,
        mesh=mesh,
        in_specs=(
            P("exp", "tok"),
            P(),
            P(),
            P("exp", None, "tok"),
            P("exp", None, "tok"),
            P("exp", None, "tok"),
        ),
        out_specs=P("exp", "tok"),
        check_vma=False,
    )
```

```python
import jax
import jax.numpy as jnp
from jax import lax
from jax.experimental import pallas as pl
from jax.experimental.pallas import tpu as pltpu
from jax.sharding import PartitionSpec as P

BLOCK = 128
SPAN = 4
CHIPS = 16
DEPTH = 16
OWNERS = 32
LINES = [[z * OWNERS + 2 * chip + core for z in range(DEPTH) for core in range(2)] for chip in range(CHIPS)]
SAME_CORE = [[2 * chip + core for chip in range(CHIPS)] for core in range(2)]
TAIL = 8
TOP = 14.0
CORE, EXPERT, HALF = 4, 5, 6


def swap_across(value):
    return lax.ppermute(value, "exp", [(p, p ^ 2) for p in range(OWNERS)])


def swap_core(value):
    return lax.ppermute(value, "exp", [(p, p ^ 1) for p in range(OWNERS)])


def encode(value, largest):
    exponent = jnp.ceil(jnp.log2(jnp.maximum(largest, 1e-30)))
    scaled = (value.astype(jnp.float32) * jnp.exp2(TOP - exponent)).astype(jnp.float16)
    tail = jnp.broadcast_to(exponent.astype(jnp.float16), (TAIL, value.shape[1]))
    return jnp.concatenate([scaled, tail])


def decode(coded):
    exponent = jnp.max(coded[..., -TAIL:, :], axis=-2, keepdims=True).astype(jnp.float32)
    value = coded[..., :-TAIL, :].astype(jnp.float32) * jnp.exp2(exponent - TOP)
    return value.astype(jnp.bfloat16)


def start_rows(sources, held, arrived):
    taken = held.shape[2]
    copies = []
    for number in range(DEPTH):
        for which, weight in enumerate(sources):
            rows = weight.at[pl.ds(number * taken, taken), :]
            copies.append(pltpu.make_async_copy(rows, held.at[number, which], arrived.at[number, which]))
            copies[-1].start()
    return copies


def product(gathered, copies, held, join):
    count = held.shape[1]
    total = None
    for number in range(DEPTH):
        for copy in copies[number * count : (number + 1) * count]:
            copy.wait()
        right = jnp.concatenate([held[number, which] for which in range(count)], axis=join)
        term = jnp.dot(gathered[number], right, preferred_element_type=jnp.float32)
        total = term if total is None else total + term
    return total


def hidden_kernel(facts, gathered, *refs):
    weights, (out, largest, held, arrived) = refs[:-4], refs[-4:]
    copies = start_rows([weight.at[kind] for kind in range(2) for weight in weights], held, arrived)
    total = product(gathered, copies, held, 1)
    units = total.shape[1] // 2
    gate, up = total[:, :units], total[:, units:]
    hidden = gate / (1.0 + jnp.exp(-gate)) * up
    out[...] = hidden.astype(out.dtype)
    largest[...] = jnp.max(jnp.abs(hidden), axis=0, keepdims=True)


def down_kernel(facts, gathered, scales, *refs):
    weights, (kept, given, held, arrived) = refs[:-4], refs[-4:]
    copies = start_rows(weights, held, arrived)
    total = product(gathered, copies, held, 0)
    count = total.shape[0]
    columns = pl.ds(pl.multiple_of(facts[HALF] * count, count), count)
    scale = jnp.broadcast_to(scales[pl.ds(facts[EXPERT], 1), columns], (128, count)).T
    total = total * scale[:, :1]
    kept[...] = total
    given[...] = total.astype(given.dtype)


def place_kernel(facts, kept, taken, out):
    out[...] = jnp.zeros_like(out)
    count = kept.shape[0]
    for pick in range(count):
        block = facts[pick]

        @pl.when(lax.rem(block, 2) == facts[CORE])
        def _():
            both = kept[pick] + taken[pick].astype(jnp.float32)
            out[pl.ds(lax.div(block, 2), 1)] = both.astype(out.dtype)[None]


def array_of(*shape):
    return jax.ShapeDtypeStruct(shape, jnp.bfloat16)


def kernel_call(kernel, name, facts, inner, outs, flops, weights=(), rows=None):
    in_vmem = pl.BlockSpec(memory_space=pltpu.VMEM)
    scratch = []
    if weights:
        count = sum(weight.size for weight in weights) // (DEPTH * rows * weights[0].shape[-1])
        scratch = [
            pltpu.VMEM((DEPTH, count, rows, weights[0].shape[-1]), jnp.bfloat16),
            pltpu.SemaphoreType.DMA((DEPTH, count)),
        ]
    return pl.pallas_call(
        kernel,
        out_shape=outs,
        in_specs=[pl.BlockSpec(memory_space=pltpu.SMEM)]
        + [in_vmem] * len(inner)
        + [pl.BlockSpec(memory_space=pltpu.HBM)] * len(weights),
        out_specs=[in_vmem] * len(outs),
        scratch_shapes=scratch,
        compiler_params=pltpu.CompilerParams(vmem_limit_bytes=24 << 20),
        cost_estimate=pl.CostEstimate(
            flops=flops, bytes_accessed=2 * sum(array.size for array in [*inner, *weights]), transcendentals=0
        ),
        name=name,
    )(facts, *inner, *[pltpu.with_memory_space_constraint(weight, pltpu.HBM) for weight in weights])


def shards(tokens, picked_blocks, gate_scale, w_gate, w_up, w_down):
    position = lax.axis_index("exp")
    core = lax.rem(position, 2)
    expert = position // SPAN
    features, units = tokens.shape[1], w_gate.shape[2]
    chosen = lax.dynamic_index_in_dim(picked_blocks, expert, 0, keepdims=False)
    side = lax.rem(position, SPAN) // 2
    half = chosen.shape[0] // 2
    rows = half * BLOCK
    picks = lax.dynamic_slice_in_dim(chosen, half * side, half)
    mine = lax.dynamic_slice_in_dim(picks, half // 2 * core, half // 2)
    facts = jnp.concatenate([picks, jnp.stack([core, expert, side]).astype(jnp.int32)])

    in_own, down_own = jnp.stack([w_gate[0], w_up[0]]), w_down[0]
    largest = jnp.max(jnp.abs(tokens.astype(jnp.float32)), axis=0, keepdims=True)
    coded, facts, mine = lax.optimization_barrier((encode(tokens, largest), facts, mine))
    held = lax.all_gather(coded, "exp")
    held, in_sent, down_sent = lax.optimization_barrier((held, in_own, down_own))
    in_far, down_far = swap_across(in_sent), swap_across(down_sent)
    gathered = lax.all_gather(held[mine], ("tok", "exp"), axis_index_groups=LINES)
    gathered, in_far = lax.optimization_barrier((gathered, in_far))
    gathered = decode(gathered).reshape(DEPTH, rows, features)
    flops = 2 * rows * DEPTH * features * SPAN * units
    hidden, largest = kernel_call(
        hidden_kernel, "hidden", facts, [gathered],
        [array_of(rows, 2 * units), jax.ShapeDtypeStruct((1, 2 * units), jnp.float32)], flops, [in_own, in_far], features,
    )
    gathered = lax.all_gather(encode(hidden, largest)[None], "tok", tiled=True)
    kept, given = kernel_call(
        down_kernel, "down", facts, [decode(gathered), gate_scale],
        [jax.ShapeDtypeStruct((rows, features), jnp.float32), array_of(rows, features)], flops // 2,
        [down_own, down_far], units,
    )

    whole = (half, BLOCK, features)
    (outgoing,) = kernel_call(
        place_kernel, "place", facts, [kept.reshape(whole), swap_core(given).reshape(whole)],
        [array_of(CHIPS, BLOCK, features)], 0,
    )
    arrived = lax.all_to_all(outgoing, "exp", 0, 0, axis_index_groups=SAME_CORE, tiled=True)
    return jnp.sum(arrived, axis=0, dtype=jnp.float32).astype(jnp.bfloat16)


def solution(mesh):
    return jax.shard_map(
        shards,
        mesh=mesh,
        in_specs=(
            P("exp", "tok"),
            P(),
            P(),
            P("exp", None, "tok"),
            P("exp", None, "tok"),
            P("exp", None, "tok"),
        ),
        out_specs=P("exp", "tok"),
        check_vma=False,
    )
```

```python
import jax
import jax.numpy as jnp
from jax import lax
from jax.experimental import pallas as pl
from jax.experimental.pallas import tpu as pltpu
from jax.sharding import PartitionSpec as P

BLOCK = 128
SPAN = 4
CHIPS = 16
DEPTH = 16
OWNERS = 32
LINES = [[z * OWNERS + 2 * chip + core for z in range(DEPTH) for core in range(2)] for chip in range(CHIPS)]
SAME_CORE = [[2 * chip + core for chip in range(CHIPS)] for core in range(2)]
TAIL = 8
TOP = 14.0
CORE, EXPERT, HALF = 4, 5, 6


def swap_across(value):
    return lax.ppermute(value, "exp", [(p, p ^ 2) for p in range(OWNERS)])


def swap_core(value):
    return lax.ppermute(value, "exp", [(p, p ^ 1) for p in range(OWNERS)])


def encode(value, largest):
    exponent = jnp.ceil(jnp.log2(jnp.maximum(largest, 1e-30)))
    scaled = (value.astype(jnp.float32) * jnp.exp2(TOP - exponent)).astype(jnp.float16)
    tail = jnp.broadcast_to(exponent.astype(jnp.float16), (TAIL, value.shape[1]))
    return jnp.concatenate([scaled, tail])


def decode(coded):
    exponent = jnp.max(coded[..., -TAIL:, :], axis=-2, keepdims=True).astype(jnp.float32)
    value = coded[..., :-TAIL, :].astype(jnp.float32) * jnp.exp2(exponent - TOP)
    return value.astype(jnp.bfloat16)


def hidden_kernel(facts, gathered, *refs):
    weights, (out, largest) = refs[:-2], refs[-2:]
    depth = gathered.shape[2]
    total = None
    for number in range(DEPTH):
        rows = pl.ds(number * depth, depth)
        right = jnp.concatenate([weight[kind, rows, :] for kind in range(2) for weight in weights], axis=1)
        term = jnp.dot(gathered[number], right, preferred_element_type=jnp.float32)
        total = term if total is None else total + term
    units = total.shape[1] // 2
    gate, up = total[:, :units], total[:, units:]
    hidden = gate / (1.0 + jnp.exp(-gate)) * up
    out[...] = hidden.astype(out.dtype)
    largest[...] = jnp.max(jnp.abs(hidden), axis=0, keepdims=True)


def down_kernel(facts, gathered, scales, *refs):
    weights, (kept, given) = refs[:-2], refs[-2:]
    depth = gathered.shape[2] // len(weights)
    total = None
    for number in range(DEPTH):
        rows = pl.ds(number * depth, depth)
        right = jnp.concatenate([weight[rows, :] for weight in weights], axis=0)
        term = jnp.dot(gathered[number], right, preferred_element_type=jnp.float32)
        total = term if total is None else total + term
    count = total.shape[0]
    columns = pl.ds(pl.multiple_of(facts[HALF] * count, count), count)
    scale = jnp.broadcast_to(scales[pl.ds(facts[EXPERT], 1), columns], (128, count)).T
    total = total * scale[:, :1]
    kept[...] = total
    given[...] = total.astype(given.dtype)


def place_kernel(facts, kept, taken, out):
    out[...] = jnp.zeros_like(out)
    count = kept.shape[0]
    for pick in range(count):
        block = facts[pick]

        @pl.when(lax.rem(block, 2) == facts[CORE])
        def _():
            both = kept[pick] + taken[pick].astype(jnp.float32)
            out[pl.ds(lax.div(block, 2), 1)] = both.astype(out.dtype)[None]


def array_of(*shape):
    return jax.ShapeDtypeStruct(shape, jnp.bfloat16)


def kernel_call(kernel, name, facts, inner, outs, flops):
    in_vmem = pl.BlockSpec(memory_space=pltpu.VMEM)
    return pl.pallas_call(
        kernel,
        out_shape=outs,
        in_specs=[pl.BlockSpec(memory_space=pltpu.SMEM)] + [in_vmem] * len(inner),
        out_specs=[in_vmem] * len(outs),
        compiler_params=pltpu.CompilerParams(vmem_limit_bytes=24 << 20),
        cost_estimate=pl.CostEstimate(
            flops=flops, bytes_accessed=2 * sum(array.size for array in inner), transcendentals=0
        ),
        name=name,
    )(facts, *inner)


def shards(tokens, picked_blocks, gate_scale, w_gate, w_up, w_down):
    position = lax.axis_index("exp")
    core = lax.rem(position, 2)
    expert = position // SPAN
    features, units = tokens.shape[1], w_gate.shape[2]
    chosen = lax.dynamic_index_in_dim(picked_blocks, expert, 0, keepdims=False)
    side = lax.rem(position, SPAN) // 2
    half = chosen.shape[0] // 2
    rows = half * BLOCK
    picks = lax.dynamic_slice_in_dim(chosen, half * side, half)
    mine = lax.dynamic_slice_in_dim(picks, half // 2 * core, half // 2)
    facts = jnp.concatenate([picks, jnp.stack([core, expert, side]).astype(jnp.int32)])

    in_own, down_own = jnp.stack([w_gate[0], w_up[0]]), w_down[0]
    largest = jnp.max(jnp.abs(tokens.astype(jnp.float32)), axis=0, keepdims=True)
    coded, facts, mine = lax.optimization_barrier((encode(tokens, largest), facts, mine))
    picked = lax.all_gather(coded, "exp")[mine]
    picked, in_sent, down_sent = lax.optimization_barrier((picked, in_own, down_own))
    in_far, down_far = swap_across(in_sent), swap_across(down_sent)
    gathered = lax.all_gather(picked, ("tok", "exp"), axis_index_groups=LINES)
    gathered, in_far = lax.optimization_barrier((gathered, in_far))
    gathered = decode(gathered).reshape(DEPTH, rows, features)
    flops = 2 * rows * DEPTH * features * SPAN * units
    hidden, largest = kernel_call(
        hidden_kernel, "hidden", facts, [gathered, in_own, in_far],
        [array_of(rows, 2 * units), jax.ShapeDtypeStruct((1, 2 * units), jnp.float32)], flops,
    )
    gathered = lax.all_gather(encode(hidden, largest)[None], "tok", tiled=True)
    kept, given = kernel_call(
        down_kernel, "down", facts, [decode(gathered), gate_scale, down_own, down_far],
        [jax.ShapeDtypeStruct((rows, features), jnp.float32), array_of(rows, features)], flops // 2,
    )

    whole = (half, BLOCK, features)
    (outgoing,) = kernel_call(
        place_kernel, "place", facts, [kept.reshape(whole), swap_core(given).reshape(whole)],
        [array_of(CHIPS, BLOCK, features)], 0,
    )
    arrived = lax.all_to_all(outgoing, "exp", 0, 0, axis_index_groups=SAME_CORE, tiled=True)
    return jnp.sum(arrived, axis=0, dtype=jnp.float32).astype(jnp.bfloat16)


def solution(mesh):
    return jax.shard_map(
        shards,
        mesh=mesh,
        in_specs=(
            P("exp", "tok"),
            P(),
            P(),
            P("exp", None, "tok"),
            P("exp", None, "tok"),
            P("exp", None, "tok"),
        ),
        out_specs=P("exp", "tok"),
        check_vma=False,
    )
```

```python
import jax
import jax.numpy as jnp
from jax import lax
from jax.experimental import pallas as pl
from jax.experimental.pallas import tpu as pltpu
from jax.sharding import PartitionSpec as P

BLOCK = 128
SPAN = 4
CHIPS = 16
DEPTH = 16
OWNERS = 32
LINES = [[z * OWNERS + 2 * chip + core for z in range(DEPTH) for core in range(2)] for chip in range(CHIPS)]
SAME_CORE = [[2 * chip + core for chip in range(CHIPS)] for core in range(2)]
TAIL = 8
TOP = 14.0
CORE, EXPERT, HALF = 4, 5, 6


def swap_across(value):
    return lax.ppermute(value, "exp", [(p, p ^ 2) for p in range(OWNERS)])


def swap_core(value):
    return lax.ppermute(value, "exp", [(p, p ^ 1) for p in range(OWNERS)])


def encode(value, largest):
    exponent = jnp.ceil(jnp.log2(jnp.maximum(largest, 1e-30)))
    scaled = (value.astype(jnp.float32) * jnp.exp2(TOP - exponent)).astype(jnp.float16)
    tail = jnp.broadcast_to(exponent.astype(jnp.float16), (TAIL, value.shape[1]))
    return jnp.concatenate([scaled, tail])


def decode(coded):
    exponent = jnp.max(coded[..., -TAIL:, :], axis=-2, keepdims=True).astype(jnp.float32)
    value = coded[..., :-TAIL, :].astype(jnp.float32) * jnp.exp2(exponent - TOP)
    return value.astype(jnp.bfloat16)


def hidden_kernel(facts, gathered, *refs):
    weights, (out, largest) = refs[:-2], refs[-2:]
    depth = gathered.shape[2]
    total = None
    for number in range(DEPTH):
        rows = pl.ds(number * depth, depth)
        right = jnp.concatenate([weight[rows, :] for weight in weights], axis=1)
        term = jnp.dot(gathered[number], right, preferred_element_type=jnp.float32)
        total = term if total is None else total + term
    units = total.shape[1] // 2
    gate, up = total[:, :units], total[:, units:]
    hidden = gate / (1.0 + jnp.exp(-gate)) * up
    out[...] = hidden.astype(out.dtype)
    largest[...] = jnp.max(jnp.abs(hidden), axis=0, keepdims=True)


def down_kernel(facts, gathered, scales, *refs):
    weights, (kept, given) = refs[:-2], refs[-2:]
    depth = gathered.shape[2] // len(weights)
    total = None
    for number in range(DEPTH):
        rows = pl.ds(number * depth, depth)
        right = jnp.concatenate([weight[rows, :] for weight in weights], axis=0)
        term = jnp.dot(gathered[number], right, preferred_element_type=jnp.float32)
        total = term if total is None else total + term
    count = total.shape[0]
    columns = pl.ds(pl.multiple_of(facts[HALF] * count, count), count)
    scale = jnp.broadcast_to(scales[pl.ds(facts[EXPERT], 1), columns], (128, count)).T
    total = total * scale[:, :1]
    kept[...] = total
    given[...] = total.astype(given.dtype)


def place_kernel(facts, kept, taken, out):
    out[...] = jnp.zeros_like(out)
    count = kept.shape[0]
    for pick in range(count):
        block = facts[pick]

        @pl.when(lax.rem(block, 2) == facts[CORE])
        def _():
            both = kept[pick] + taken[pick].astype(jnp.float32)
            out[pl.ds(lax.div(block, 2), 1)] = both.astype(out.dtype)[None]


def array_of(*shape):
    return jax.ShapeDtypeStruct(shape, jnp.bfloat16)


def kernel_call(kernel, name, facts, inner, outs, flops):
    in_vmem = pl.BlockSpec(memory_space=pltpu.VMEM)
    return pl.pallas_call(
        kernel,
        out_shape=outs,
        in_specs=[pl.BlockSpec(memory_space=pltpu.SMEM)] + [in_vmem] * len(inner),
        out_specs=[in_vmem] * len(outs),
        compiler_params=pltpu.CompilerParams(vmem_limit_bytes=24 << 20),
        cost_estimate=pl.CostEstimate(
            flops=flops, bytes_accessed=2 * sum(array.size for array in inner), transcendentals=0
        ),
        name=name,
    )(facts, *inner)


def shards(tokens, picked_blocks, gate_scale, w_gate, w_up, w_down):
    position = lax.axis_index("exp")
    core = lax.rem(position, 2)
    expert = position // SPAN
    features, units = tokens.shape[1], w_gate.shape[2]
    chosen = lax.dynamic_index_in_dim(picked_blocks, expert, 0, keepdims=False)
    side = lax.rem(position, SPAN) // 2
    half = chosen.shape[0] // 2
    rows = half * BLOCK
    picks = lax.dynamic_slice_in_dim(chosen, half * side, half)
    mine = lax.dynamic_slice_in_dim(picks, half // 2 * core, half // 2)
    facts = jnp.concatenate([picks, jnp.stack([core, expert, side]).astype(jnp.int32)])

    own = [w_gate[0], w_up[0], w_down[0]]
    largest = jnp.max(jnp.abs(tokens.astype(jnp.float32)), axis=0, keepdims=True)
    coded, facts, mine = lax.optimization_barrier((encode(tokens, largest), facts, mine))
    picked = lax.all_gather(coded, "exp")[mine]
    picked, sent = lax.optimization_barrier((picked, own))
    far = [swap_across(weight) for weight in sent]
    gathered = lax.all_gather(picked, ("tok", "exp"), axis_index_groups=LINES)
    gathered, far[:2] = lax.optimization_barrier((gathered, far[:2]))
    gathered = decode(gathered).reshape(DEPTH, rows, features)
    flops = 2 * rows * DEPTH * features * SPAN * units
    hidden, largest = kernel_call(
        hidden_kernel, "hidden", facts, [gathered, own[0], far[0], own[1], far[1]],
        [array_of(rows, 2 * units), jax.ShapeDtypeStruct((1, 2 * units), jnp.float32)], flops,
    )
    gathered = lax.all_gather(encode(hidden, largest)[None], "tok", tiled=True)
    kept, given = kernel_call(
        down_kernel, "down", facts, [decode(gathered), gate_scale, own[2], far[2]],
        [jax.ShapeDtypeStruct((rows, features), jnp.float32), array_of(rows, features)], flops // 2,
    )

    whole = (half, BLOCK, features)
    (outgoing,) = kernel_call(
        place_kernel, "place", facts, [kept.reshape(whole), swap_core(given).reshape(whole)],
        [array_of(CHIPS, BLOCK, features)], 0,
    )
    arrived = lax.all_to_all(outgoing, "exp", 0, 0, axis_index_groups=SAME_CORE, tiled=True)
    return jnp.sum(arrived, axis=0, dtype=jnp.float32).astype(jnp.bfloat16)


def solution(mesh):
    return jax.shard_map(
        shards,
        mesh=mesh,
        in_specs=(
            P("exp", "tok"),
            P(),
            P(),
            P("exp", None, "tok"),
            P("exp", None, "tok"),
            P("exp", None, "tok"),
        ),
        out_specs=P("exp", "tok"),
        check_vma=False,
    )
```

```python
import jax
import jax.numpy as jnp
from jax import lax
from jax.experimental import pallas as pl
from jax.experimental.pallas import tpu as pltpu
from jax.sharding import PartitionSpec as P

BLOCK = 128
SPAN = 4
CHIPS = 16
DEPTH = 16
OWNERS = 32
LINES = [[z * OWNERS + 2 * chip + core for z in range(DEPTH) for core in range(2)] for chip in range(CHIPS)]
SAME_CORE = [[2 * chip + core for chip in range(CHIPS)] for core in range(2)]
TAIL = 8
TOP = 14.0
CORE, EXPERT, HALF = 4, 5, 6


def swap_across(value):
    return lax.ppermute(value, "exp", [(p, p ^ 2) for p in range(OWNERS)])


def swap_core(value):
    return lax.ppermute(value, "exp", [(p, p ^ 1) for p in range(OWNERS)])


def encode(value, largest):
    exponent = jnp.ceil(jnp.log2(jnp.maximum(largest, 1e-30)))
    scaled = (value.astype(jnp.float32) * jnp.exp2(TOP - exponent)).astype(jnp.float16)
    tail = jnp.broadcast_to(exponent.astype(jnp.float16), (TAIL, value.shape[1]))
    return jnp.concatenate([scaled, tail])


def decode(coded):
    exponent = jnp.max(coded[..., -TAIL:, :], axis=-2, keepdims=True).astype(jnp.float32)
    value = coded[..., :-TAIL, :].astype(jnp.float32) * jnp.exp2(exponent - TOP)
    return value.astype(jnp.bfloat16)


def hidden_kernel(facts, gathered, *refs):
    weights, (out, largest) = refs[:-2], refs[-2:]
    depth = gathered.shape[2]
    total = None
    for number in range(DEPTH):
        rows = pl.ds(number * depth, depth)
        right = jnp.concatenate([weight[rows, :] for weight in weights], axis=1)
        term = jnp.dot(gathered[number], right, preferred_element_type=jnp.float32)
        total = term if total is None else total + term
    units = total.shape[1] // 2
    gate, up = total[:, :units], total[:, units:]
    hidden = gate / (1.0 + jnp.exp(-gate)) * up
    out[...] = hidden.astype(out.dtype)
    largest[...] = jnp.max(jnp.abs(hidden), axis=0, keepdims=True)


def down_kernel(facts, gathered, scales, *refs):
    weights, (kept, given) = refs[:-2], refs[-2:]
    depth = gathered.shape[2] // len(weights)
    total = None
    for number in range(DEPTH):
        rows = pl.ds(number * depth, depth)
        right = jnp.concatenate([weight[rows, :] for weight in weights], axis=0)
        term = jnp.dot(gathered[number], right, preferred_element_type=jnp.float32)
        total = term if total is None else total + term
    count = total.shape[0]
    columns = pl.ds(pl.multiple_of(facts[HALF] * count, count), count)
    scale = jnp.broadcast_to(scales[pl.ds(facts[EXPERT], 1), columns], (128, count)).T
    total = total * scale[:, :1]
    kept[...] = total
    given[...] = total.astype(given.dtype)


def place_kernel(facts, kept, taken, out):
    out[...] = jnp.zeros_like(out)
    count = kept.shape[0]
    for pick in range(count):
        block = facts[pick]

        @pl.when(lax.rem(block, 2) == facts[CORE])
        def _():
            both = kept[pick] + taken[pick].astype(jnp.float32)
            out[pl.ds(lax.div(block, 2), 1)] = both.astype(out.dtype)[None]


def array_of(*shape):
    return jax.ShapeDtypeStruct(shape, jnp.bfloat16)


def kernel_call(kernel, name, facts, inner, outs, flops):
    in_vmem = pl.BlockSpec(memory_space=pltpu.VMEM)
    return pl.pallas_call(
        kernel,
        out_shape=outs,
        in_specs=[pl.BlockSpec(memory_space=pltpu.SMEM)] + [in_vmem] * len(inner),
        out_specs=[in_vmem] * len(outs),
        compiler_params=pltpu.CompilerParams(vmem_limit_bytes=24 << 20),
        cost_estimate=pl.CostEstimate(
            flops=flops, bytes_accessed=2 * sum(array.size for array in inner), transcendentals=0
        ),
        name=name,
    )(facts, *inner)


def shards(tokens, picked_blocks, gate_scale, w_gate, w_up, w_down):
    position = lax.axis_index("exp")
    core = lax.rem(position, 2)
    expert = position // SPAN
    features, units = tokens.shape[1], w_gate.shape[2]
    chosen = lax.dynamic_index_in_dim(picked_blocks, expert, 0, keepdims=False)
    side = lax.rem(position, SPAN) // 2
    half = chosen.shape[0] // 2
    rows = half * BLOCK
    picks = lax.dynamic_slice_in_dim(chosen, half * side, half)
    mine = lax.dynamic_slice_in_dim(picks, half // 2 * core, half // 2)
    facts = jnp.concatenate([picks, jnp.stack([core, expert, side]).astype(jnp.int32)])

    own = [w_gate[0], w_up[0], w_down[0]]
    largest = jnp.max(jnp.abs(tokens.astype(jnp.float32)), axis=0, keepdims=True)
    coded, facts, mine = lax.optimization_barrier((encode(tokens, largest), facts, mine))
    picked = lax.all_gather(coded, "exp")[mine]
    picked, *sent = lax.optimization_barrier((picked, *own[:2]))
    far = [swap_across(weight) for weight in sent]
    gathered = lax.all_gather(picked, ("tok", "exp"), axis_index_groups=LINES)
    gathered, far, down_sent = lax.optimization_barrier((gathered, far, own[2]))
    far.append(swap_across(down_sent))
    gathered = decode(gathered).reshape(DEPTH, rows, features)
    flops = 2 * rows * DEPTH * features * SPAN * units
    hidden, largest = kernel_call(
        hidden_kernel, "hidden", facts, [gathered, own[0], far[0], own[1], far[1]],
        [array_of(rows, 2 * units), jax.ShapeDtypeStruct((1, 2 * units), jnp.float32)], flops,
    )
    gathered = lax.all_gather(encode(hidden, largest)[None], "tok", tiled=True)
    kept, given = kernel_call(
        down_kernel, "down", facts, [decode(gathered), gate_scale, own[2], far[2]],
        [jax.ShapeDtypeStruct((rows, features), jnp.float32), array_of(rows, features)], flops // 2,
    )

    whole = (half, BLOCK, features)
    (outgoing,) = kernel_call(
        place_kernel, "place", facts, [kept.reshape(whole), swap_core(given).reshape(whole)],
        [array_of(CHIPS, BLOCK, features)], 0,
    )
    arrived = lax.all_to_all(outgoing, "exp", 0, 0, axis_index_groups=SAME_CORE, tiled=True)
    return jnp.sum(arrived, axis=0, dtype=jnp.float32).astype(jnp.bfloat16)


def solution(mesh):
    return jax.shard_map(
        shards,
        mesh=mesh,
        in_specs=(
            P("exp", "tok"),
            P(),
            P(),
            P("exp", None, "tok"),
            P("exp", None, "tok"),
            P("exp", None, "tok"),
        ),
        out_specs=P("exp", "tok"),
        check_vma=False,
    )
```

```python
import jax
import jax.numpy as jnp
from jax import lax
from jax.experimental import pallas as pl
from jax.experimental.pallas import tpu as pltpu
from jax.sharding import PartitionSpec as P

BLOCK = 128
SPAN = 4
CHIPS = 16
DEPTH = 16
OWNERS = 32
LINES = [[z * OWNERS + 2 * chip + core for z in range(DEPTH) for core in range(2)] for chip in range(CHIPS)]
SAME_CORE = [[2 * chip + core for chip in range(CHIPS)] for core in range(2)]
TAIL = 8
TOP = 14.0
CORE, EXPERT, HALF = 4, 5, 6


def swap_across(value):
    return lax.ppermute(value, "exp", [(p, p ^ 2) for p in range(OWNERS)])


def swap_core(value):
    return lax.ppermute(value, "exp", [(p, p ^ 1) for p in range(OWNERS)])


def encode(value, largest):
    exponent = jnp.ceil(jnp.log2(jnp.maximum(largest, 1e-30)))
    scaled = (value.astype(jnp.float32) * jnp.exp2(TOP - exponent)).astype(jnp.float16)
    tail = jnp.broadcast_to(exponent.astype(jnp.float16), (TAIL, value.shape[1]))
    return jnp.concatenate([scaled, tail])


def decode(coded):
    exponent = jnp.max(coded[..., -TAIL:, :], axis=-2, keepdims=True).astype(jnp.float32)
    value = coded[..., :-TAIL, :].astype(jnp.float32) * jnp.exp2(exponent - TOP)
    return value.astype(jnp.bfloat16)


def hidden_kernel(facts, gathered, *refs):
    weights, (out, largest) = refs[:-2], refs[-2:]
    depth = gathered.shape[2]
    total = None
    for number in range(DEPTH):
        rows = pl.ds(number * depth, depth)
        right = jnp.concatenate([weight[kind, rows, :] for kind in range(2) for weight in weights], axis=1)
        term = jnp.dot(gathered[number], right, preferred_element_type=jnp.float32)
        total = term if total is None else total + term
    units = total.shape[1] // 2
    gate, up = total[:, :units], total[:, units:]
    hidden = gate / (1.0 + jnp.exp(-gate)) * up
    out[...] = hidden.astype(out.dtype)
    largest[...] = jnp.max(jnp.abs(hidden), axis=0, keepdims=True)


def down_kernel(facts, gathered, scales, *refs):
    weights, (kept, given) = refs[:-2], refs[-2:]
    depth = gathered.shape[2] // len(weights)
    total = None
    for number in range(DEPTH):
        rows = pl.ds(number * depth, depth)
        right = jnp.concatenate([weight[rows, :] for weight in weights], axis=0)
        term = jnp.dot(gathered[number], right, preferred_element_type=jnp.float32)
        total = term if total is None else total + term
    count = total.shape[0]
    columns = pl.ds(pl.multiple_of(facts[HALF] * count, count), count)
    scale = jnp.broadcast_to(scales[pl.ds(facts[EXPERT], 1), columns], (128, count)).T
    total = total * scale[:, :1]
    kept[...] = total
    given[...] = total.astype(given.dtype)


def place_kernel(facts, kept, taken, out):
    out[...] = jnp.zeros_like(out)
    count = kept.shape[0]
    for pick in range(count):
        block = facts[pick]

        @pl.when(lax.rem(block, 2) == facts[CORE])
        def _():
            both = kept[pick] + taken[pick].astype(jnp.float32)
            out[pl.ds(lax.div(block, 2), 1)] = both.astype(out.dtype)[None]


def array_of(*shape):
    return jax.ShapeDtypeStruct(shape, jnp.bfloat16)


def kernel_call(kernel, name, facts, inner, outs, flops):
    in_vmem = pl.BlockSpec(memory_space=pltpu.VMEM)
    return pl.pallas_call(
        kernel,
        out_shape=outs,
        in_specs=[pl.BlockSpec(memory_space=pltpu.SMEM)] + [in_vmem] * len(inner),
        out_specs=[in_vmem] * len(outs),
        compiler_params=pltpu.CompilerParams(vmem_limit_bytes=24 << 20),
        cost_estimate=pl.CostEstimate(
            flops=flops, bytes_accessed=2 * sum(array.size for array in inner), transcendentals=0
        ),
        name=name,
    )(facts, *inner)


def shards(tokens, picked_blocks, gate_scale, w_gate, w_up, w_down):
    position = lax.axis_index("exp")
    core = lax.rem(position, 2)
    expert = position // SPAN
    features, units = tokens.shape[1], w_gate.shape[2]
    chosen = lax.dynamic_index_in_dim(picked_blocks, expert, 0, keepdims=False)
    side = lax.rem(position, SPAN) // 2
    half = chosen.shape[0] // 2
    rows = half * BLOCK
    picks = lax.dynamic_slice_in_dim(chosen, half * side, half)
    mine = lax.dynamic_slice_in_dim(picks, half // 2 * core, half // 2)
    facts = jnp.concatenate([picks, jnp.stack([core, expert, side]).astype(jnp.int32)])

    largest = jnp.max(jnp.abs(tokens.astype(jnp.float32)), axis=0, keepdims=True)
    coded, facts, mine = lax.optimization_barrier((encode(tokens, largest), facts, mine))
    picked = lax.all_gather(coded, "exp")[mine]
    picked, w_gate, w_up, w_down = lax.optimization_barrier((picked, w_gate, w_up, w_down))
    in_own, down_own = jnp.stack([w_gate[0], w_up[0]]), w_down[0]
    in_far, down_far = swap_across(in_own), swap_across(down_own)
    gathered = lax.all_gather(picked, ("tok", "exp"), axis_index_groups=LINES)
    gathered, in_far = lax.optimization_barrier((gathered, in_far))
    gathered = decode(gathered).reshape(DEPTH, rows, features)
    flops = 2 * rows * DEPTH * features * SPAN * units
    hidden, largest = kernel_call(
        hidden_kernel, "hidden", facts, [gathered, in_own, in_far],
        [array_of(rows, 2 * units), jax.ShapeDtypeStruct((1, 2 * units), jnp.float32)], flops,
    )
    gathered = lax.all_gather(encode(hidden, largest)[None], "tok", tiled=True)
    kept, given = kernel_call(
        down_kernel, "down", facts, [decode(gathered), gate_scale, down_own, down_far],
        [jax.ShapeDtypeStruct((rows, features), jnp.float32), array_of(rows, features)], flops // 2,
    )

    whole = (half, BLOCK, features)
    (outgoing,) = kernel_call(
        place_kernel, "place", facts, [kept.reshape(whole), swap_core(given).reshape(whole)],
        [array_of(CHIPS, BLOCK, features)], 0,
    )
    arrived = lax.all_to_all(outgoing, "exp", 0, 0, axis_index_groups=SAME_CORE, tiled=True)
    return jnp.sum(arrived, axis=0, dtype=jnp.float32).astype(jnp.bfloat16)


def solution(mesh):
    return jax.shard_map(
        shards,
        mesh=mesh,
        in_specs=(
            P("exp", "tok"),
            P(),
            P(),
            P("exp", None, "tok"),
            P("exp", None, "tok"),
            P("exp", None, "tok"),
        ),
        out_specs=P("exp", "tok"),
        check_vma=False,
    )
```

```python
import jax
import jax.numpy as jnp
from jax import lax
from jax.experimental import pallas as pl
from jax.experimental.pallas import tpu as pltpu
from jax.sharding import PartitionSpec as P

BLOCK = 128
SPAN = 4
CHIPS = 16
DEPTH = 16
OWNERS = 32
LINES = [[z * OWNERS + 2 * chip + core for z in range(DEPTH) for core in range(2)] for chip in range(CHIPS)]
SAME_CORE = [[2 * chip + core for chip in range(CHIPS)] for core in range(2)]
TAIL = 8
TOP = 14.0
CORE, EXPERT, HALF = 4, 5, 6


def swap_across(value):
    return lax.ppermute(value, "exp", [(p, p ^ 2) for p in range(OWNERS)])


def swap_core(value):
    return lax.ppermute(value, "exp", [(p, p ^ 1) for p in range(OWNERS)])


def encode(value, largest):
    exponent = jnp.ceil(jnp.log2(jnp.maximum(largest, 1e-30)))
    scaled = (value.astype(jnp.float32) * jnp.exp2(TOP - exponent)).astype(jnp.float16)
    tail = jnp.broadcast_to(exponent.astype(jnp.float16), (TAIL, value.shape[1]))
    return jnp.concatenate([scaled, tail])


def decode(coded):
    exponent = jnp.max(coded[..., -TAIL:, :], axis=-2, keepdims=True).astype(jnp.float32)
    value = coded[..., :-TAIL, :].astype(jnp.float32) * jnp.exp2(exponent - TOP)
    return value.astype(jnp.bfloat16)


def hidden_kernel(facts, gathered, *refs):
    weights, (out, largest) = refs[:-2], refs[-2:]
    depth = gathered.shape[2]
    total = None
    for number in range(DEPTH):
        rows = pl.ds(number * depth, depth)
        right = jnp.concatenate([weight[rows, :] for weight in weights], axis=1)
        term = jnp.dot(gathered[number], right, preferred_element_type=jnp.float32)
        total = term if total is None else total + term
    units = total.shape[1] // 2
    gate, up = total[:, :units], total[:, units:]
    hidden = gate / (1.0 + jnp.exp(-gate)) * up
    out[...] = hidden.astype(out.dtype)
    largest[...] = jnp.max(jnp.abs(hidden), axis=0, keepdims=True)


def down_kernel(facts, gathered, scales, *refs):
    weights, (kept, given) = refs[:-2], refs[-2:]
    depth = gathered.shape[2] // len(weights)
    total = None
    for number in range(DEPTH):
        rows = pl.ds(number * depth, depth)
        right = jnp.concatenate([weight[rows, :] for weight in weights], axis=0)
        term = jnp.dot(gathered[number], right, preferred_element_type=jnp.float32)
        total = term if total is None else total + term
    count = total.shape[0]
    columns = pl.ds(pl.multiple_of(facts[HALF] * count, count), count)
    scale = jnp.broadcast_to(scales[pl.ds(facts[EXPERT], 1), columns], (128, count)).T
    total = total * scale[:, :1]
    kept[...] = total
    given[...] = total.astype(given.dtype)


def place_kernel(facts, kept, taken, out):
    out[...] = jnp.zeros_like(out)
    count = kept.shape[0]
    for pick in range(count):
        block = facts[pick]

        @pl.when(lax.rem(block, 2) == facts[CORE])
        def _():
            both = kept[pick] + taken[pick].astype(jnp.float32)
            out[pl.ds(lax.div(block, 2), 1)] = both.astype(out.dtype)[None]


def arrive_kernel(picks, owner, arrived, out):
    found, first, second = jnp.int32(0), jnp.int32(0), jnp.int32(0)
    experts, count = picks.shape
    for expert in range(experts):
        for pick in range(count):
            chip = 2 * expert + pick // (count // 2)
            hit = picks[expert, pick] == owner[0]
            first = jnp.where(hit & (found == 0), chip, first)
            second = jnp.where(hit & (found == 1), chip, second)
            found = jnp.where(hit, found + 1, found)
    both = arrived[pl.ds(first, 1)].astype(jnp.float32) + arrived[pl.ds(second, 1)].astype(jnp.float32)
    out[...] = both[0].astype(out.dtype)


def array_of(*shape):
    return jax.ShapeDtypeStruct(shape, jnp.bfloat16)


def kernel_call(kernel, name, facts, inner, outs, flops):
    in_vmem = pl.BlockSpec(memory_space=pltpu.VMEM)
    return pl.pallas_call(
        kernel,
        out_shape=outs,
        in_specs=[pl.BlockSpec(memory_space=pltpu.SMEM)] + [in_vmem] * len(inner),
        out_specs=[in_vmem] * len(outs),
        compiler_params=pltpu.CompilerParams(vmem_limit_bytes=24 << 20),
        cost_estimate=pl.CostEstimate(
            flops=flops, bytes_accessed=2 * sum(array.size for array in inner), transcendentals=0
        ),
        name=name,
    )(facts, *inner)


def shards(tokens, picked_blocks, gate_scale, w_gate, w_up, w_down):
    position = lax.axis_index("exp")
    core = lax.rem(position, 2)
    expert = position // SPAN
    features, units = tokens.shape[1], w_gate.shape[2]
    chosen = lax.dynamic_index_in_dim(picked_blocks, expert, 0, keepdims=False)
    side = lax.rem(position, SPAN) // 2
    half = chosen.shape[0] // 2
    rows = half * BLOCK
    picks = lax.dynamic_slice_in_dim(chosen, half * side, half)
    mine = lax.dynamic_slice_in_dim(picks, half // 2 * core, half // 2)
    facts = jnp.concatenate([picks, jnp.stack([core, expert, side]).astype(jnp.int32)])

    own = [w_gate[0], w_up[0], w_down[0]]
    largest = jnp.max(jnp.abs(tokens.astype(jnp.float32)), axis=0, keepdims=True)
    owner = position.astype(jnp.int32).reshape(1)
    coded, facts, mine, owner = lax.optimization_barrier((encode(tokens, largest), facts, mine, owner))
    picked = lax.all_gather(coded, "exp")[mine]
    picked, sent = lax.optimization_barrier((picked, own))
    far = [swap_across(weight) for weight in sent]
    gathered = lax.all_gather(picked, ("tok", "exp"), axis_index_groups=LINES)
    gathered, far[:2] = lax.optimization_barrier((gathered, far[:2]))
    gathered = decode(gathered).reshape(DEPTH, rows, features)
    flops = 2 * rows * DEPTH * features * SPAN * units
    hidden, largest = kernel_call(
        hidden_kernel, "hidden", facts, [gathered, own[0], far[0], own[1], far[1]],
        [array_of(rows, 2 * units), jax.ShapeDtypeStruct((1, 2 * units), jnp.float32)], flops,
    )
    gathered = lax.all_gather(encode(hidden, largest)[None], "tok", tiled=True)
    kept, given = kernel_call(
        down_kernel, "down", facts, [decode(gathered), gate_scale, own[2], far[2]],
        [jax.ShapeDtypeStruct((rows, features), jnp.float32), array_of(rows, features)], flops // 2,
    )

    whole = (half, BLOCK, features)
    (outgoing,) = kernel_call(
        place_kernel, "place", facts, [kept.reshape(whole), swap_core(given).reshape(whole)],
        [array_of(CHIPS, BLOCK, features)], 0,
    )
    arrived = lax.all_to_all(outgoing, "exp", 0, 0, axis_index_groups=SAME_CORE, tiled=True)
    in_smem, in_vmem = pl.BlockSpec(memory_space=pltpu.SMEM), pl.BlockSpec(memory_space=pltpu.VMEM)
    return pl.pallas_call(
        arrive_kernel,
        out_shape=array_of(BLOCK, features),
        in_specs=[in_smem, in_smem, in_vmem],
        out_specs=in_vmem,
        name="arrive",
    )(picked_blocks, owner, pltpu.with_memory_space_constraint(arrived, pltpu.VMEM))


def solution(mesh):
    return jax.shard_map(
        shards,
        mesh=mesh,
        in_specs=(
            P("exp", "tok"),
            P(),
            P(),
            P("exp", None, "tok"),
            P("exp", None, "tok"),
            P("exp", None, "tok"),
        ),
        out_specs=P("exp", "tok"),
        check_vma=False,
    )
```

```python
import jax
import jax.numpy as jnp
from jax import lax
from jax.experimental import pallas as pl
from jax.experimental.pallas import tpu as pltpu
from jax.sharding import PartitionSpec as P

BLOCK = 128
SPAN = 4
CHIPS = 16
DEPTH = 16
OWNERS = 32
LINES = [[z * OWNERS + 2 * chip + core for z in range(DEPTH) for core in range(2)] for chip in range(CHIPS)]
SAME_CORE = [[2 * chip + core for chip in range(CHIPS)] for core in range(2)]
TAIL = 8
TOP = 14.0
CORE, EXPERT, HALF = 4, 5, 6


def swap_across(value):
    return lax.ppermute(value, "exp", [(p, p ^ 2) for p in range(OWNERS)])


def swap_core(value):
    return lax.ppermute(value, "exp", [(p, p ^ 1) for p in range(OWNERS)])


def encode(value, largest):
    exponent = jnp.ceil(jnp.log2(jnp.maximum(largest, 1e-30)))
    scaled = (value.astype(jnp.float32) * jnp.exp2(TOP - exponent)).astype(jnp.float16)
    tail = jnp.broadcast_to(exponent.astype(jnp.float16), (TAIL, value.shape[1]))
    return jnp.concatenate([scaled, tail])


def decode(coded):
    exponent = jnp.max(coded[..., -TAIL:, :], axis=-2, keepdims=True).astype(jnp.float32)
    value = coded[..., :-TAIL, :].astype(jnp.float32) * jnp.exp2(exponent - TOP)
    return value.astype(jnp.bfloat16)


def hidden_kernel(facts, gathered, *refs):
    weights, (out, largest) = refs[:-2], refs[-2:]
    depth = gathered.shape[2]
    total = None
    for number in range(DEPTH):
        rows = pl.ds(number * depth, depth)
        right = jnp.concatenate([weight[rows, :] for weight in weights], axis=1)
        term = jnp.dot(gathered[number], right, preferred_element_type=jnp.float32)
        total = term if total is None else total + term
    units = total.shape[1] // 2
    gate, up = total[:, :units], total[:, units:]
    hidden = gate / (1.0 + jnp.exp(-gate)) * up
    out[...] = hidden.astype(out.dtype)
    largest[...] = jnp.max(jnp.abs(hidden), axis=0, keepdims=True)


def down_kernel(facts, gathered, scales, *refs):
    weights, (kept, given) = refs[:-2], refs[-2:]
    depth = gathered.shape[2] // len(weights)
    total = None
    for number in range(DEPTH):
        rows = pl.ds(number * depth, depth)
        right = jnp.concatenate([weight[rows, :] for weight in weights], axis=0)
        term = jnp.dot(gathered[number], right, preferred_element_type=jnp.float32)
        total = term if total is None else total + term
    count = total.shape[0]
    columns = pl.ds(pl.multiple_of(facts[HALF] * count, count), count)
    scale = jnp.broadcast_to(scales[pl.ds(facts[EXPERT], 1), columns], (128, count)).T
    total = total * scale[:, :1]
    kept[...] = total
    given[...] = total.astype(given.dtype)


def place_kernel(facts, kept, taken, out):
    out[...] = jnp.zeros_like(out)
    count = kept.shape[0]
    for pick in range(count):
        block = facts[pick]

        @pl.when(lax.rem(block, 2) == facts[CORE])
        def _():
            both = kept[pick] + taken[pick].astype(jnp.float32)
            out[pl.ds(lax.div(block, 2), 1)] = both.astype(out.dtype)[None]


def array_of(*shape):
    return jax.ShapeDtypeStruct(shape, jnp.bfloat16)


def kernel_call(kernel, name, facts, inner, outs, flops):
    in_vmem = pl.BlockSpec(memory_space=pltpu.VMEM)
    return pl.pallas_call(
        kernel,
        out_shape=outs,
        in_specs=[pl.BlockSpec(memory_space=pltpu.SMEM)] + [in_vmem] * len(inner),
        out_specs=[in_vmem] * len(outs),
        compiler_params=pltpu.CompilerParams(vmem_limit_bytes=24 << 20),
        cost_estimate=pl.CostEstimate(
            flops=flops, bytes_accessed=2 * sum(array.size for array in inner), transcendentals=0
        ),
        name=name,
    )(facts, *inner)


def shards(tokens, picked_blocks, gate_scale, w_gate, w_up, w_down):
    position = lax.axis_index("exp")
    core = lax.rem(position, 2)
    expert = position // SPAN
    features, units = tokens.shape[1], w_gate.shape[2]
    chosen = lax.dynamic_index_in_dim(picked_blocks, expert, 0, keepdims=False)
    side = lax.rem(position, SPAN) // 2
    half = chosen.shape[0] // 2
    rows = half * BLOCK
    picks = lax.dynamic_slice_in_dim(chosen, half * side, half)
    mine = lax.dynamic_slice_in_dim(picks, half // 2 * core, half // 2)
    facts = jnp.concatenate([picks, jnp.stack([core, expert, side]).astype(jnp.int32)])

    own = [w_gate[0], w_up[0], w_down[0]]
    largest = jnp.max(jnp.abs(tokens.astype(jnp.float32)), axis=0, keepdims=True)
    coded, facts, mine = lax.optimization_barrier((encode(tokens, largest), facts, mine))
    picked = lax.all_gather(coded, "exp")[mine]
    picked, sent = lax.optimization_barrier((picked, own))
    far = [swap_across(weight) for weight in sent]
    gathered = lax.all_gather(picked, ("tok", "exp"), axis_index_groups=LINES)
    gathered, far[:2] = lax.optimization_barrier((gathered, far[:2]))
    gathered = decode(gathered).reshape(DEPTH, rows, features)
    flops = 2 * rows * DEPTH * features * SPAN * units
    hidden, largest = kernel_call(
        hidden_kernel, "hidden", facts, [gathered, own[0], far[0], own[1], far[1]],
        [array_of(rows, 2 * units), jax.ShapeDtypeStruct((1, 2 * units), jnp.float32)], flops,
    )
    coded = jnp.stack([encode(part, largest) for part in jnp.split(hidden, 2)])
    gathered = lax.all_gather(coded, "tok")
    kept, given = kernel_call(
        down_kernel, "down", facts, [decode(gathered).reshape(DEPTH, rows, 2 * units), gate_scale, own[2], far[2]],
        [jax.ShapeDtypeStruct((rows, features), jnp.float32), array_of(rows, features)], flops // 2,
    )

    whole = (half, BLOCK, features)
    (outgoing,) = kernel_call(
        place_kernel, "place", facts, [kept.reshape(whole), swap_core(given).reshape(whole)],
        [array_of(CHIPS, BLOCK, features)], 0,
    )
    arrived = lax.all_to_all(outgoing, "exp", 0, 0, axis_index_groups=SAME_CORE, tiled=True)
    return jnp.sum(arrived, axis=0, dtype=jnp.float32).astype(jnp.bfloat16)


def solution(mesh):
    return jax.shard_map(
        shards,
        mesh=mesh,
        in_specs=(
            P("exp", "tok"),
            P(),
            P(),
            P("exp", None, "tok"),
            P("exp", None, "tok"),
            P("exp", None, "tok"),
        ),
        out_specs=P("exp", "tok"),
        check_vma=False,
    )
```
